256 devices in a mesh: ctx: 32 (over y, x, core), head: 8 (over z).
Axes of the slice: x: 4, y: 4, z: 8, core: 2. Of those that a mesh axis runs over, the one named last changes fastest.
Arguments:
- queries: bfloat16 [16384, 4096], P('ctx', 'head'), may hold values from -6 to 6
- keys: bfloat16 [16384, 4096], P('ctx', 'head'), may hold values from -6 to 6
- values: bfloat16 [16384, 4096], P('ctx', 'head'), may hold values from -6 to 6
- log_decay: float32 [32, 16384], P('head', 'ctx'), may hold values from -2 to 0
- level_pick: int32 [32, 16384], P('head', 'ctx'), may hold values from 0 to 15
- level_table: float32 [32, 8, 16], P('head'), may hold values from 0.2 to 2
- out_weight: bfloat16 [4096, 8192], P('head', 'ctx'), may hold values from -0.1875 to 0.1875
Outputs:
- layer_out: bfloat16 [16384, 8192], P('ctx', 'head')
The draws below stay inside these ranges and needn't reach their ends.
All inputs are finite; a program needn't handle non-finite values.
Results may differ from the reference program's by a relative error of at most 0.024.
Values may be sent and summed in bfloat16 or wider, within the bound.
A program may use at most 128 MiB of HBM per device.

```python
import math
import jax
import jax.numpy as jnp
from jax import lax

D = 8192
LOCAL_HEADS = 32
HD = 128
BLOCK = 128
TABLE = 16
TOK_DEV = 512
WINDOW_TOKENS = 16384
HL = 4
LEVELS = 8
N_HEAD = 8


def draw_log_decay(key, part):
    key_sequence = jax.random.split(key, 6)
    slow_share = 0.5
    is_slow = jax.random.uniform(key_sequence[0], (LOCAL_HEADS, 1)) < slow_share
    fast_rate = jnp.exp(jax.random.uniform(key_sequence[1], (LOCAL_HEADS, 1), minval=math.log(1.0 / 50.0), maxval=math.log(1.0 / 30.0)))
    base_rate = jnp.where(is_slow, 0.6 / WINDOW_TOKENS, fast_rate)
    device_factor = jnp.exp(jax.random.uniform(key_sequence[2], (LOCAL_HEADS, WINDOW_TOKENS // TOK_DEV), minval=math.log(0.5), maxval=math.log(2.0)))
    device_factor = jnp.repeat(device_factor, TOK_DEV, axis=1)
    token_factor = jax.random.uniform(key_sequence[3], (LOCAL_HEADS, WINDOW_TOKENS), minval=0.5, maxval=2.0)
    run_offsets = jax.random.randint(key_sequence[4], (3, 1), 0, WINDOW_TOKENS)
    run_lengths = jax.random.uniform(key_sequence[5], (LOCAL_HEADS, 3), minval=math.log(0.55), maxval=math.log(0.8))
    token_positions = lax.broadcasted_iota(jnp.int32, (3, WINDOW_TOKENS), 1)
    match_count = (token_positions == run_offsets).astype(jnp.float32)
    final_output = -base_rate * device_factor * token_factor
    for token_run in range(3):
        final_output = final_output + run_lengths[:, token_run:token_run + 1] * match_count[token_run][None, :]
    return final_output.astype(jnp.float32)


def set_ends(result, stream_key, low, high):
    shape = result.shape
    spot = [jax.random.randint(jax.random.fold_in(stream_key, axis), (), 0, shape[axis]) for axis in range(len(shape))]
    result = result.at[tuple(spot)].set(low)
    longest = shape.index(max(shape))
    spot[longest] = (spot[longest] + 1) % shape[longest]
    return result.at[tuple(spot)].set(high)


def with_spikes(values, stream_key, source, target, parts, factor):
    owner, partner = [(jnp.arange(values.shape[axis_at]) // (values.shape[axis_at] // parts)).reshape([-1 if axis == axis_at else 1 for axis in range(values.ndim)]) for axis_at in (source, target)]
    chosen = jax.random.permutation(stream_key, parts)[partner]
    strong = (owner == chosen) | (owner == (partner + parts // 2) % parts)
    return jnp.where(strong, factor * values, values)


def levels(key, extent, cuts, smallest, largest):
    def one(dim, blocks):
        heights = jax.random.uniform(jax.random.fold_in(jax.random.fold_in(key, 6), dim), (blocks,), jnp.float32, smallest / len(cuts), largest / len(cuts))
        return jnp.repeat(jnp.exp(heights), extent[dim] // blocks).reshape((-1,) + (1,) * (len(extent) - dim - 1))

    level = one(*cuts[0])
    for cut in cuts[1:]:
        level = level * one(*cut)
    return level


def gaussian(rng, dims, scale, reach, cuts=(), kind=jnp.bfloat16):
    loudness = levels(rng, dims, cuts, -0.22, 0.18) if cuts else 1.0
    drawn = jax.random.normal(rng, dims, jnp.float32) * scale * loudness
    return jnp.minimum(jnp.maximum(drawn, -reach), reach).astype(kind)


def noise_with(own_key, dims, scale, reach, cuts, heavy, kind=jnp.bfloat16):
    drawn = scale * jax.random.normal(own_key, dims, jnp.float32)
    if cuts:
        drawn = drawn * levels(own_key, dims, cuts, -0.22, 0.18)
    return jnp.clip(with_spikes(drawn, jax.random.fold_in(own_key, 3), *heavy), -reach, reach).astype(kind)


def setup_inputs(seed: int = 0) -> dict:
    key_list = jax.random.split(jax.random.key(seed), 8)
    return {
        "queries": gaussian(key_list[0], (WINDOW_TOKENS, LOCAL_HEADS * HD), 1.0, 6.0, ((0, 32), (1, 8))),
        "keys": gaussian(key_list[1], (WINDOW_TOKENS, LOCAL_HEADS * HD), 1.0, 6.0, ((0, 32), (1, 8))),
        "values": gaussian(key_list[2], (WINDOW_TOKENS, LOCAL_HEADS * HD), 1.0, 6.0, ((0, 32), (1, 8))),
        "log_decay": draw_log_decay(jax.random.fold_in(key_list[7], 71), 0),
        "level_pick": set_ends(jax.random.randint(key_list[4], (LOCAL_HEADS, WINDOW_TOKENS), 0, TABLE), jax.random.fold_in(key_list[4], 1), 0, TABLE - 1).astype(jnp.int32),
        "level_table": jnp.clip(jnp.exp(math.log(2.0) - 2.3025851 * jax.random.uniform(key_list[5], (LOCAL_HEADS, LEVELS, TABLE), jnp.float32) ** levels(key_list[5], (LOCAL_HEADS, LEVELS, TABLE), ((0, 8),), -0.2, 0.2)), 0.2, 2.0),
        "out_weight": noise_with(key_list[6], (LOCAL_HEADS * HD, D), (LOCAL_HEADS * HD) ** -0.5, 0.1875, ((0, 8), (1, 32)), (0, 1, 32, 2.75)),
    }


def head_attention(inputs):
    query, head_keys, head_values, log_rate, pick, table = inputs
    blocks = WINDOW_TOKENS // BLOCK
    query3 = query.reshape(blocks, BLOCK, HD).astype(jnp.float32)
    keys3 = head_keys.reshape(blocks, BLOCK, HD).astype(jnp.float32)
    values3 = head_values.reshape(blocks, BLOCK, HD).astype(jnp.float32)
    within = jnp.cumsum(log_rate.reshape(blocks, BLOCK), axis=1)
    block_decay = within[:, -1]
    block_end = jnp.cumsum(block_decay)
    block_start = block_end - block_decay
    level_weight = table[:, pick].reshape(LEVELS, blocks, BLOCK)
    scores = jnp.einsum('cti,csi->cts', query3, keys3)
    rows = lax.broadcasted_iota(jnp.int32, (BLOCK, BLOCK), 0)
    cols = lax.broadcasted_iota(jnp.int32, (BLOCK, BLOCK), 1)
    causal = (rows >= cols)[None]
    log_gaps = within[:, :, None] - within[:, None, :]
    decays = jnp.where(causal, jnp.exp(jnp.where(causal, log_gaps, 0.0)), 0.0)
    weights = (level_weight[0][:, :, None] * decays * scores).astype(jnp.bfloat16)
    mixture = jnp.einsum('cts,csi->cti', weights.astype(jnp.float32), values3)
    block_keys = (keys3 * jnp.exp(block_decay[:, None] - within)[:, :, None]).astype(jnp.bfloat16)
    block_state = jnp.einsum('csi,csj->cij', block_keys.astype(jnp.float32), values3)
    numbers = jnp.arange(blocks, dtype=jnp.int32)
    for level in range(LEVELS - 1):
        upper_end = numbers >> level << level
        bit_set = numbers >> level & 1 == 1
        inside = bit_set[:, None] & (numbers[None, :] >= (upper_end - (1 << level))[:, None]) & (numbers[None, :] < upper_end[:, None])
        factors = jnp.where(inside, jnp.exp(jnp.where(inside, block_start[:, None] - block_end[None, :], 0.0)), 0.0)
        level_state = jnp.einsum('cm,mij->cij', factors, block_state, precision=lax.Precision.HIGHEST)
        level_rounded = level_state.astype(jnp.bfloat16)
        level_queries = (level_weight[1 + level][:, :, None] * jnp.exp(within)[:, :, None] * query3).astype(jnp.bfloat16)
        mixture = mixture + jnp.einsum('cti,cij->ctj', level_queries.astype(jnp.float32), level_rounded.astype(jnp.float32))
    mixture = mixture.reshape(WINDOW_TOKENS, HD)
    normed = mixture * lax.rsqrt(lax.optimization_barrier(jnp.mean(mixture * mixture, axis=-1, keepdims=True)) + 1e-06)
    return normed.astype(jnp.bfloat16)

def reference(queries, keys, values, log_decay, level_pick, level_table, out_weight):
    query_heads = jnp.transpose(queries.reshape(WINDOW_TOKENS, LOCAL_HEADS, HD), (1, 0, 2))
    key_heads = jnp.transpose(keys.reshape(WINDOW_TOKENS, LOCAL_HEADS, HD), (1, 0, 2))
    value_heads = jnp.transpose(values.reshape(WINDOW_TOKENS, LOCAL_HEADS, HD), (1, 0, 2))
    normed = lax.map(head_attention, (query_heads, key_heads, value_heads, log_decay, level_pick, level_table))
    flattened = jnp.transpose(normed, (1, 0, 2)).reshape(WINDOW_TOKENS, LOCAL_HEADS * HD)
    width = HL * HD
    total = jnp.zeros((WINDOW_TOKENS, D), jnp.float32)
    for group in range(N_HEAD):
        group_out = jnp.dot(flattened[:, group * width:(group + 1) * width], out_weight[group * width:(group + 1) * width], preferred_element_type=jnp.float32).astype(jnp.bfloat16)
        total = total + group_out.astype(jnp.float32)
    return total.astype(jnp.bfloat16)
```

```python
import functools
import math

import jax
import jax.numpy as jnp
from jax import lax
from jax.experimental import pallas as pl
from jax.experimental.pallas import tpu as pltpu
from jax.sharding import PartitionSpec as P

HD = 128
BLOCK = 128
HL = 4
TOK = 512
NB = TOK // BLOCK
COLS = 256
MESH = pl.DeviceIdType.MESH
BF = jnp.bfloat16
F32 = jnp.float32


def kernel(
    X, Y, Z,
    q_ref, k_ref, v_ref, ld_ref, pick_ref, table_ref, w_ref, out_ref,
    qb, kb, vb, picks, wrows, bdrows, col, mix, lst, t0, t0p, d0, d0p, fall, xb, xd, yb, yd, rs, rb, ab, wb, acc, ob,
    in_sem, out_sem, w0s, w0r, w1s, w1r, w2s, w2r, wcs, wcr, cs, cr, xs, xr, ys, yr, rss, rsr, rings, ringr,
):
    R = X * Y
    RP = TOK // R
    xbits = X.bit_length() - 1
    ybits = Y.bit_length() - 1
    NR = 1 + xbits + ybits
    me = lax.axis_index("ctx")
    z = lax.axis_index("head")
    c = lax.rem(me, 2)
    chip = me // 2
    x = lax.rem(chip, X)
    y = chip // X
    plane = me // 4
    half = lax.rem(x, 2)
    mate = (me + 1 - 2 * c, z)
    right = lax.rem(z + 1, Z)
    left = lax.rem(z + Z - 1, Z)

    def at_x(step):
        return (y * X + lax.rem(x + step, X)) * 2 + c

    def at_y(step):
        return (lax.rem(y + step, Y) * X + x) * 2 + c

    def remote(src, dst, ssem, rsem, dev):
        return pltpu.make_async_remote_copy(
            src_ref=src, dst_ref=dst, send_sem=ssem, recv_sem=rsem, device_id=dev, device_id_type=MESH
        )

    loads = []
    for n, (src, dst) in enumerate(((k_ref, kb), (v_ref, vb), (q_ref, qb))):
        for h in range(HL):
            cp = pltpu.make_async_copy(src.at[:, h * HD:(h + 1) * HD], dst.at[h], in_sem.at[n, h])
            cp.start()
            loads.append(cp)

    barrier = pltpu.get_barrier_semaphore()

    def greet(ctx, head):
        pl.semaphore_signal(barrier, inc=1, device_id=(ctx, head), device_id_type=MESH)

    greet(mate[0], z)
    for s in range(1, X):
        greet(at_x(s), z)
    for s in range(1, Y):
        greet(at_y(s), z)
    greet(me, right)
    greet(me, left)

    def greet_sources(n, carry):
        ctx = 4 * z + 2 * (n // Z) + c
        head = lax.rem(n, Z)

        @pl.when(jnp.logical_or(ctx != me, head != z))
        def _():
            greet(ctx, head)

        return carry

    lax.fori_loop(0, 2 * Z, greet_sources, 0)

    for b in range(NB):
        wrows[b * HL:(b + 1) * HL, :] = ld_ref[:, b * BLOCK:(b + 1) * BLOCK]
        picks[b * HL:(b + 1) * HL, :] = pick_ref[:, b * BLOCK:(b + 1) * BLOCK]
    run = wrows[...]
    lane = lax.broadcasted_iota(jnp.int32, run.shape, 1)
    step = 1
    while step < BLOCK:
        run = run + jnp.where(lane >= step, pltpu.roll(run, step, 1), 0.0)
        step *= 2
    wrows[...] = run
    bdrows[...] = jnp.broadcast_to(run[:, BLOCK - 1:BLOCK], run.shape)
    d0[...] = jnp.zeros_like(d0)
    sub = lax.broadcasted_iota(jnp.int32, (8, BLOCK), 0)

    def prepare(h, carry):
        tab = table_ref[h]
        bd = [bdrows[pl.ds(b * HL + h, 1), :] for b in range(NB)]
        start = jnp.zeros_like(bd[0])
        rows = []
        for b in range(NB):
            pk = jnp.broadcast_to(picks[pl.ds(b * HL + h, 1), :], (8, BLOCK))
            lw = jnp.zeros((8, BLOCK), F32)
            for n in range(16):
                lw = jnp.where(pk == n, tab[:, n:n + 1], lw)
            wr = wrows[pl.ds(b * HL + h, 1), :]
            upper = jnp.where(sub >= 3, start, 0.0)
            if b == 3:
                upper = jnp.where(sub == 2, bd[2], upper)
            rows.append(lw * jnp.where(sub == 0, 1.0, jnp.exp(wr + upper)))
            rows.append(jnp.where(sub == 0, wr, jnp.where(sub == 1, jnp.exp(bd[b] - wr), 0.0)))
            start = start + bd[b]
        rows.append(jnp.zeros((BLOCK - 16 * NB, BLOCK), F32))
        col[h] = jnp.concatenate(rows, axis=0).T
        d0[pl.ds(h, 1), :] = start
        return carry

    lax.fori_loop(0, HL, prepare, 0)

    same = (plane == z).astype(jnp.int32)
    pl.semaphore_wait(barrier, 1 + (X - 1) + (Y - 1) + 2 + R - same)

    def w0_copy(r):
        return remote(
            w_ref.at[pl.ds(r * RP, RP), :],
            wb.at[r // X, lax.rem(r, X), c, half, z],
            w0s.at[r], w0r.at[half, z], (r * 2 + c, plane),
        )

    def w0_own():
        return pltpu.make_async_copy(
            w_ref.at[pl.ds(chip * RP, RP), :], wb.at[y, x, c, half, z], w0r.at[half, z]
        )

    def w0_send(n, carry):
        r = lax.rem(chip + 1 + n, R)
        own = jnp.logical_and(r == chip, plane == z)

        @pl.when(own)
        def _():
            w0_own().start()

        @pl.when(jnp.logical_not(own))
        def _():
            w0_copy(r).start()

        return carry

    lax.fori_loop(0, R, w0_send, 0)

    for cp in loads[:2 * HL]:
        cp.wait()

    def states(h, carry):
        s = []
        for b in range(NB):
            kk = kb[h, b * BLOCK:(b + 1) * BLOCK, :].astype(F32)
            kk = (kk * col[h, :, b * 16 + 9:b * 16 + 10]).astype(BF)
            s.append(lax.dot_general(
                kk, vb[h, b * BLOCK:(b + 1) * BLOCK, :], (((0,), (0,)), ((), ())), preferred_element_type=F32
            ))
        e = [jnp.exp(bdrows[pl.ds(b * HL + h, 1), :]) for b in range(NB)]
        pair = e[1] * s[0] + s[1]
        lst[h, 0] = s[0].astype(BF)
        lst[h, 1] = pair.astype(BF)
        lst[h, 2] = s[2].astype(BF)
        t0[h] = (e[3] * (e[2] * pair + s[2]) + s[3]).astype(BF)
        return carry

    lax.fori_loop(0, HL, states, 0)

    core_copies = [
        remote(t0, t0p, cs.at[0], cr.at[0], mate),
        remote(d0, d0p, cs.at[1], cr.at[1], mate),
    ]
    for cp in core_copies:
        cp.start()

    for cp in loads[2 * HL:]:
        cp.wait()
    causal = (
        lax.broadcasted_iota(jnp.int32, (BLOCK, BLOCK), 0) >= lax.broadcasted_iota(jnp.int32, (BLOCK, BLOCK), 1)
    )

    def inside(h):
        for b in range(NB):
            rows = slice(b * BLOCK, (b + 1) * BLOCK)
            qq = qb[h, rows, :]
            score = lax.dot_general(
                qq, kb[h, rows, :], (((1,), (1,)), ((), ())), preferred_element_type=F32
            )
            gap = col[h, :, b * 16 + 8:b * 16 + 9] - wrows[pl.ds(b * HL + h, 1), :]
            decay = jnp.where(causal, jnp.exp(jnp.where(causal, gap, 0.0)), 0.0)
            lhs = [(col[h, :, b * 16:b * 16 + 1] * decay * score).astype(BF)]
            rhs = [vb[h, rows, :]]
            qf = qq.astype(F32)
            if b & 1:
                lhs.append((qf * col[h, :, b * 16 + 1:b * 16 + 2]).astype(BF))
                rhs.append(lst[h, b - 1])
            if b & 2:
                lhs.append((qf * col[h, :, b * 16 + 2:b * 16 + 3]).astype(BF))
                rhs.append(lst[h, 1])
            mix[h, rows, :] = jnp.dot(
                jnp.concatenate(lhs, axis=1), jnp.concatenate(rhs, axis=0), preferred_element_type=F32
            )

    inside(0)

    for cp in core_copies:
        cp.wait_recv()
    first = jnp.exp(jnp.where(c == 0, d0[...], d0p[...]))
    second = jnp.exp(jnp.where(c == 0, d0p[...], d0[...]))
    d1 = d0[...] + d0p[...]
    xd[x] = d1
    fall[0] = first
    fall[1] = second
    for n in range(2):
        h = 2 * c + n
        sec = fall[1, pl.ds(h, 1), :]
        mine = t0[h].astype(F32) * jnp.where(c == 0, sec, 1.0)
        other = t0p[h].astype(F32) * jnp.where(c == 0, 1.0, sec)
        xb[x, n] = (mine + other).astype(BF)
    x_copies = []
    for s in range(1, X):
        dev = (at_x(s), z)
        src = lax.rem(x + X - s, X)
        for buf, i in ((xb, 0), (xd, 1)):
            cp = remote(buf.at[x], buf.at[x], xs.at[s - 1, i], xr.at[s - 1, i], dev)
            cp.start()
            got = remote(buf.at[src], buf.at[src], xs.at[s - 1, i], xr.at[s - 1, i], dev)
            x_copies.append((cp, got))
    for h in range(HL):
        rb[h, 0] = jnp.where(c == 1, t0p[h].astype(F32), 0.0).astype(BF)

    inside(1)

    for cp, got in x_copies:
        got.wait_recv()

    def weighted(buf, dec, n, at, size, before):
        h = 2 * c + n
        d = [dec[i, pl.ds(h, 1), :] for i in range(size)]
        ends, total = [], jnp.zeros_like(d[0])
        start = jnp.zeros_like(d[0])
        for i in range(size):
            start = start + jnp.where(i < at, d[i], 0.0)
            total = total + d[i]
            ends.append(total)
        f = [buf[i, n].astype(F32) for i in range(size)]
        near = [jnp.exp(jnp.minimum(start - ends[i], 0.0) + before) for i in range(size)]
        levels = []
        for bit in range(size.bit_length() - 1):
            top = (at >> bit) << bit
            low = top - (1 << bit)
            on = ((at >> bit) & 1) == 1
            part = jnp.zeros((HD, HD), F32)
            for i in range(size):
                take = jnp.logical_and(on, jnp.logical_and(i >= low, i < top))
                part = part + jnp.where(take, near[i], 0.0) * f[i]
            levels.append(part)
        whole = jnp.zeros((HD, HD), F32)
        for i in range(size):
            whole = whole + jnp.exp(total - ends[i]) * f[i]
        return levels, whole, start, total

    def keep(n, slot, value):
        h = 2 * c + n
        lower = fall[0, pl.ds(h, 1), :]
        rb[h, 1 + slot] = (value * jnp.where(c == 1, lower, 1.0)).astype(BF)
        rs[n, slot] = (value * jnp.where(c == 0, lower, 1.0)).astype(BF)

    offsets = []
    yd[y] = jnp.zeros((8, BLOCK), F32)
    for n in range(2):
        levels, whole, start, total = weighted(xb, xd, n, x, X, 0.0)
        for bit in range(xbits):
            keep(n, bit, levels[bit])
        yb[y, n] = whole.astype(BF)
        yd[y, pl.ds(2 * c + n, 1), :] = total
        offsets.append(start)
    y_copies = []
    for s in range(1, Y):
        dev = (at_y(s), z)
        src = lax.rem(y + Y - s, Y)
        for buf, i in ((yb, 0), (yd, 1)):
            cp = remote(buf.at[y], buf.at[y], ys.at[s - 1, i], yr.at[s - 1, i], dev)
            cp.start()
            got = remote(buf.at[src], buf.at[src], ys.at[s - 1, i], yr.at[s - 1, i], dev)
            y_copies.append((cp, got))

    inside(2)
    inside(3)

    for cp, got in y_copies:
        got.wait_recv()
    for n in range(2):
        levels, _, _, _ = weighted(yb, yd, n, y, Y, offsets[n])
        for bit in range(ybits):
            keep(n, xbits + bit, levels[bit])
    state_copy = remote(rs, rb.at[pl.ds(2 * c, 2), pl.ds(1, NR - 1)], rss.at[0], rsr.at[0], mate)
    state_got = remote(rs, rb.at[pl.ds(2 - 2 * c, 2), pl.ds(1, NR - 1)], rss.at[0], rsr.at[0], mate)
    state_copy.start()

    def w0_wait(n, carry):
        a, b = n // Z, lax.rem(n, Z)
        pltpu.make_async_copy(w_ref.at[pl.ds(0, RP), :], wb.at[y, x, c, a, b], w0r.at[a, b]).wait()
        return carry

    lax.fori_loop(0, 2 * Z, w0_wait, 0)
    w1 = []
    for s in range(1, X):
        piece, dev = wb.at[y, x, c, 0], (at_x(s), z)
        cp = remote(piece, piece, w1s.at[0, s - 1], w1r.at[0, s - 1], dev)
        cp.start()
        there = wb.at[y, lax.rem(x + X - s, X), c, 0]
        w1.append((cp, remote(there, there, w1s.at[0, s - 1], w1r.at[0, s - 1], dev)))
    for s in range(1, Y):
        piece, dev = wb.at[y, x, c, 1], (at_y(s), z)
        cp = remote(piece, piece, w1s.at[1, s - 1], w1r.at[1, s - 1], dev)
        cp.start()
        there = wb.at[lax.rem(y + Y - s, Y), x, c, 1]
        w1.append((cp, remote(there, there, w1s.at[1, s - 1], w1r.at[1, s - 1], dev)))

    H2 = Z // 2

    def travels(way, d, n):
        return d < H2 - 1 or (n < 2) == (way == 0)

    def ring(way, d, n):
        origin = lax.rem(z + (Z - d if way == 0 else d), Z)
        chunk = ab.at[origin, lax.rem(2 * c + n, HL)]
        dev = (me, right if way == 0 else left)
        return remote(chunk, chunk, rings.at[way, d, n], ringr.at[way, d, n], dev)

    def ring_got(way, d, n):
        origin = lax.rem(z + (Z - d - 1 if way == 0 else d + 1), Z)
        chunk = ab.at[origin, lax.rem(2 * c + n, HL)]
        dev = (me, right if way == 0 else left)
        return remote(chunk, chunk, rings.at[way, d, n], ringr.at[way, d, n], dev)

    def finish(h):
        for b in range(NB):
            rows = slice(b * BLOCK, (b + 1) * BLOCK)
            qf = qb[h, rows, :].astype(F32)
            lhs = jnp.concatenate(
                [(qf * col[h, :, b * 16 + 3 + n:b * 16 + 4 + n]).astype(BF) for n in range(NR)], axis=1
            )
            total = mix[h, rows, :] + jnp.dot(lhs, rb[h].reshape(NR * HD, HD), preferred_element_type=F32)
            mean = jnp.mean(total * total, axis=-1, keepdims=True)
            ab[z, h, rows, :] = (total * lax.rsqrt(mean + 1e-06)).astype(BF)

    for n in range(HL):
        if n == 2:
            state_got.wait_recv()
        finish(lax.rem(2 * c + n, HL))
        for way in range(2):
            if travels(way, 0, n):
                ring(way, 0, n).start()

    for cp, got in w1:
        got.wait_recv()
    w2 = []
    for s in range(1, Y):
        piece, dev = wb.at[y, :, c, 0], (at_y(s), z)
        cp = remote(piece, piece, w2s.at[0, s - 1], w2r.at[0, s - 1], dev)
        cp.start()
        there = wb.at[lax.rem(y + Y - s, Y), :, c, 0]
        w2.append((cp, remote(there, there, w2s.at[0, s - 1], w2r.at[0, s - 1], dev)))
    for s in range(1, X):
        piece, dev = wb.at[:, x, c, 1], (at_x(s), z)
        cp = remote(piece, piece, w2s.at[1, s - 1], w2r.at[1, s - 1], dev)
        cp.start()
        there = wb.at[:, lax.rem(x + X - s, X), c, 1]
        w2.append((cp, remote(there, there, w2s.at[1, s - 1], w2r.at[1, s - 1], dev)))
    wc = []

    def across(piece_of, way, s):
        cp = remote(piece_of(c), piece_of(c), wcs.at[way, s], wcr.at[way, s], mate)
        cp.start()
        other = piece_of(1 - c)
        wc.append((cp, remote(other, other, wcs.at[way, s], wcr.at[way, s], mate)))

    across(lambda core: wb.at[y, :, core, 0], 0, 0)
    across(lambda core: wb.at[:, x, core, 1], 1, 0)

    def w2_pass():
        for _, got in w2:
            got.wait_recv()
        for s in range(1, Y):
            across(lambda core: wb.at[lax.rem(y + Y - s, Y), :, core, 0], 0, s)
        for s in range(1, X):
            across(lambda core: wb.at[:, lax.rem(x + X - s, X), core, 1], 1, s)

    def project(origin, first, last=False):
        lhs = jnp.concatenate([ab[origin, h] for h in range(HL)], axis=1)

        def tile(u, carry):
            rhs = wb[:, :, lax.rem(u, 2), u // 2, origin].reshape(TOK, COLS)
            part = jnp.dot(lhs, rhs, preferred_element_type=F32)
            if not first:
                part = part + acc[u]
            if last:
                ob[u] = part.astype(BF)
                out_copy(u).start()
            else:
                acc[u] = part
            return carry

        lax.fori_loop(0, 4, tile, 0)

    def out_copy(u):
        return pltpu.make_async_copy(ob.at[u], out_ref.at[:, pl.ds(pl.multiple_of(u * COLS, COLS), COLS)], out_sem.at[u])

    waiting = [z]
    weights_here = False
    begun = False
    for d in range(H2):
        if d == H2 - 2 or (H2 == 1 and d == 0):
            w2_pass()
        for n in range(HL):
            for way in range(2):
                if travels(way, d, n):
                    ring_got(way, d, n).wait_recv()
                    if d + 1 < H2 and travels(way, d + 1, n):
                        ring(way, d + 1, n).start()
            if weights_here:
                for _ in range(2):
                    if waiting:
                        project(waiting.pop(0), not begun)
                        begun = True
            elif d >= H2 - 2:
                for cp, got in wc:
                    got.wait_recv()
                weights_here = True
        if d + 1 < H2:
            waiting.append(lax.rem(z + Z - d - 1, Z))
            waiting.append(lax.rem(z + d + 1, Z))
    while waiting:
        project(waiting.pop(0), not begun)
        begun = True
    project(lax.rem(z + H2, Z), False, True)

    def w0_sent(n, carry):
        own = jnp.logical_and(n == chip, plane == z)

        @pl.when(jnp.logical_not(own))
        def _():
            w0_copy(n).wait_send()

        return carry

    lax.fori_loop(0, R, w0_sent, 0)
    for cp in core_copies:
        cp.wait_send()
    state_copy.wait_send()
    for cp, _ in x_copies + y_copies + w1 + w2 + wc:
        cp.wait_send()
    for way in range(2):
        for d in range(H2):
            for n in range(HL):
                if travels(way, d, n):
                    ring(way, d, n).wait_send()
    for u in range(4):
        out_copy(u).wait()


def local(X, Y, Z, queries, keys, values, log_decay, level_pick, level_table, out_weight):
    R = X * Y
    NR = 1 + (X.bit_length() - 1) + (Y.bit_length() - 1)
    H2 = Z // 2
    anyspace = pl.BlockSpec(memory_space=pl.ANY)
    vmem = pl.BlockSpec(memory_space=pltpu.VMEM)
    dma = pltpu.SemaphoreType.DMA
    heads = (HL, TOK, HD)
    state = (HD, HD)
    scratch = [
        pltpu.VMEM(heads, BF), pltpu.VMEM(heads, BF), pltpu.VMEM(heads, BF),
        pltpu.VMEM((NB * HL, BLOCK), jnp.int32), pltpu.VMEM((NB * HL, BLOCK), F32), pltpu.VMEM((NB * HL, BLOCK), F32),
        pltpu.VMEM((HL, BLOCK, BLOCK), F32),
        pltpu.VMEM(heads, F32),
        pltpu.VMEM((HL, 3) + state, BF),
        pltpu.VMEM((HL,) + state, BF), pltpu.VMEM((HL,) + state, BF),
        pltpu.VMEM((8, BLOCK), F32), pltpu.VMEM((8, BLOCK), F32), pltpu.VMEM((2, 8, BLOCK), F32),
        pltpu.VMEM((X, 2) + state, BF), pltpu.VMEM((X, 8, BLOCK), F32),
        pltpu.VMEM((Y, 2) + state, BF), pltpu.VMEM((Y, 8, BLOCK), F32),
        pltpu.VMEM((2, NR - 1) + state, BF), pltpu.VMEM((HL, NR) + state, BF),
        pltpu.VMEM((Z,) + heads, BF),
        pltpu.VMEM((Y, X, 2, 2, Z, TOK // R, COLS), BF),
        pltpu.VMEM((4, TOK, COLS), F32), pltpu.VMEM((4, TOK, COLS), BF),
        dma((3, HL)), dma((4,)),
        dma((R,)), dma((2, Z)),
        dma((2, max(X, Y))), dma((2, max(X, Y))),
        dma((2, max(X, Y))), dma((2, max(X, Y))),
        dma((2, max(X, Y))), dma((2, max(X, Y))),
        dma((2,)), dma((2,)),
        dma((X, 2)), dma((X, 2)),
        dma((Y, 2)), dma((Y, 2)),
        dma((1,)), dma((1,)),
        dma((2, H2, HL)), dma((2, H2, HL)),
    ]
    return pl.pallas_call(
        functools.partial(kernel, X, Y, Z),
        out_shape=jax.ShapeDtypeStruct((TOK, 4 * COLS), BF),
        in_specs=[anyspace, anyspace, anyspace, vmem, vmem, vmem, anyspace],
        out_specs=anyspace,
        scratch_shapes=scratch,
        cost_estimate=pl.CostEstimate(flops=5_000_000_000, bytes_accessed=4_000_000, transcendentals=1_000_000),
        compiler_params=pltpu.CompilerParams(
            collective_id=0, has_side_effects=True, vmem_limit_bytes=48 * 1024 * 1024
        ),
    )(queries, keys, values, log_decay, level_pick, level_table, out_weight)


def solution(mesh):
    nctx, Z = mesh.shape["ctx"], mesh.shape["head"]
    chips = nctx // 2
    X = 1 << int(math.log2(chips)) // 2
    Y = chips // X
    in_specs = (
        P("ctx", "head"),
        P("ctx", "head"),
        P("ctx", "head"),
        P("head", "ctx"),
        P("head", "ctx"),
        P("head", None, None),
        P("head", "ctx"),
    )
    return jax.shard_map(
        functools.partial(local, X, Y, Z), mesh=mesh, in_specs=in_specs, out_specs=P("ctx", "head"), check_vma=False
    )
```

```python
import functools
import math

import jax
import jax.numpy as jnp
from jax import lax
from jax.experimental import pallas as pl
from jax.experimental.pallas import tpu as pltpu
from jax.sharding import PartitionSpec as P

HD = 128
BLOCK = 128
HL = 4
TOK = 512
NB = TOK // BLOCK
COLS = 256
W2_SLOT, W3_SLOTS = 2, (5, 7, 9)
MESH = pl.DeviceIdType.MESH
BF = jnp.bfloat16
F32 = jnp.float32


def kernel(
    X, Y, Z,
    q_ref, k_ref, v_ref, ld_hbm, pick_hbm, table_hbm, w_ref, out_ref,
    ld_ref, pick_ref, table_ref,
    qb, kb, vb, picks, wrows, bdrows, col, mix, lst, stage, t0, t0p, d0, d0p, fall, xb, xd, yb, yd, rs, rb, ab, wb, acc, ob,
    in_sem, out_sem, wqs, wqr, w0s, w0r, w1s, w1r, w2s, w2r, wcs, wcr, cs, cr, xs, xr, ys, yr, rss, rsr, rings, ringr,
):
    R = X * Y
    RP = TOK // R
    xbits = X.bit_length() - 1
    ybits = Y.bit_length() - 1
    NR = 1 + xbits + ybits
    me = lax.axis_index("ctx")
    z = lax.axis_index("head")
    c = lax.rem(me, 2)
    chip = me // 2
    x = lax.rem(chip, X)
    y = chip // X
    half = lax.rem(x, 2)
    mate = (me + 1 - 2 * c, z)
    right = lax.rem(z + 1, Z)
    left = lax.rem(z + Z - 1, Z)

    def at_x(step):
        return (y * X + lax.rem(x + step, X)) * 2 + c

    def at_y(step):
        return (lax.rem(y + step, Y) * X + x) * 2 + c

    def remote(src, dst, ssem, rsem, dev):
        return pltpu.make_async_remote_copy(
            src_ref=src, dst_ref=dst, send_sem=ssem, recv_sem=rsem, device_id=dev, device_id_type=MESH
        )

    barrier = pltpu.get_barrier_semaphore()

    def greet(ctx, head):
        pl.semaphore_signal(barrier, inc=1, device_id=(ctx, head), device_id_type=MESH)

    greet(mate[0], z)
    for s in range(1, X):
        greet(at_x(s), z)
    for s in range(1, Y):
        greet(at_y(s), z)
    greet(me, right)
    greet(me, left)

    for n in range(2):
        for head in range(Z):
            greet((y * X + 2 * lax.rem(z, 2) + n) * 2 + c, head)

    small = [
        pltpu.make_async_copy(src, dst, in_sem.at[3, n])
        for n, (src, dst) in enumerate(((ld_hbm, ld_ref), (pick_hbm, pick_ref), (table_hbm, table_ref)))
    ]
    for cp in small:
        cp.start()
    loads = []
    for n, (src, dst) in enumerate(((k_ref, kb), (v_ref, vb), (q_ref, qb))):
        for h in range(HL):
            cp = pltpu.make_async_copy(src.at[:, h * HD:(h + 1) * HD], dst.at[h], in_sem.at[n, h])
            cp.start()
            loads.append(cp)

    for cp in small:
        cp.wait()

    for b in range(NB):
        wrows[b * HL:(b + 1) * HL, :] = ld_ref[:, b * BLOCK:(b + 1) * BLOCK]
        picks[b * HL:(b + 1) * HL, :] = pick_ref[:, b * BLOCK:(b + 1) * BLOCK]
    run = wrows[...]
    lane = lax.broadcasted_iota(jnp.int32, run.shape, 1)
    step = 1
    while step < BLOCK:
        run = run + jnp.where(lane >= step, pltpu.roll(run, step, 1), 0.0)
        step *= 2
    wrows[...] = run
    bdrows[...] = jnp.broadcast_to(run[:, BLOCK - 1:BLOCK], run.shape)
    d0[...] = jnp.zeros_like(d0)
    sub = lax.broadcasted_iota(jnp.int32, (8, BLOCK), 0)

    def prepare(h, carry):
        tab = table_ref[h]
        bd = [bdrows[pl.ds(b * HL + h, 1), :] for b in range(NB)]
        start = jnp.zeros_like(bd[0])
        rows = []
        for b in range(NB):
            pk = jnp.broadcast_to(picks[pl.ds(b * HL + h, 1), :], (8, BLOCK))
            lw = jnp.zeros((8, BLOCK), F32)
            for n in range(16):
                lw = jnp.where(pk == n, tab[:, n:n + 1], lw)
            wr = wrows[pl.ds(b * HL + h, 1), :]
            upper = jnp.where(sub >= 3, start, 0.0)
            if b == 3:
                upper = jnp.where(sub == 2, bd[2], upper)
            rows.append(lw * jnp.where(sub == 0, 1.0, jnp.exp(wr + upper)))
            rows.append(jnp.where(sub == 0, wr, jnp.where(sub == 1, jnp.exp(bd[b] - wr), 0.0)))
            start = start + bd[b]
        rows.append(jnp.zeros((BLOCK - 16 * NB, BLOCK), F32))
        col[h] = jnp.concatenate(rows, axis=0).T
        d0[pl.ds(h, 1), :] = start
        return carry

    lax.fori_loop(0, HL, prepare, 0)

    for cp in loads[:2 * HL]:
        cp.wait()

    def states(h, carry):
        s = []
        for b in range(NB):
            kk = kb[h, b * BLOCK:(b + 1) * BLOCK, :].astype(F32)
            kk = (kk * col[h, :, b * 16 + 9:b * 16 + 10]).astype(BF)
            s.append(lax.dot_general(
                kk, vb[h, b * BLOCK:(b + 1) * BLOCK, :], (((0,), (0,)), ((), ())), preferred_element_type=F32
            ))
        e = [jnp.exp(bdrows[pl.ds(b * HL + h, 1), :]) for b in range(NB)]
        pair = e[1] * s[0] + s[1]
        lst[h, 0] = s[0].astype(BF)
        lst[h, 1] = pair.astype(BF)
        lst[h, 2] = s[2].astype(BF)
        t0[h] = (e[3] * (e[2] * pair + s[2]) + s[3]).astype(BF)
        return carry

    lax.fori_loop(0, HL, states, 0)

    pl.semaphore_wait(barrier, 1 + (X - 1) + (Y - 1) + 2 + R)

    QR = TOK // Y

    def w_quarter(row):
        return w_ref.at[pl.ds(pl.multiple_of(row * QR, QR), QR), :]

    wq = [pltpu.make_async_copy(w_quarter(y), stage.at[y], wqr.at[0])]
    wq_got = [wq[0]]
    for s in range(1, Y):
        dev = (at_y(s), z)
        src = lax.rem(y + Y - s, Y)
        wq.append(remote(w_quarter(lax.rem(y + s, Y)), stage.at[y], wqs.at[s], wqr.at[s], dev))
        wq_got.append(remote(w_quarter(y), stage.at[src], wqs.at[s], wqr.at[s], dev))
    for cp in wq:
        cp.start()

    def w0_place(n):
        row, col_at = lax.rem(n // X + y, Y), lax.rem(n + x, X)
        plane = 2 * row + x // 2
        return row, col_at, plane, jnp.logical_and(plane == z, col_at == x)

    def w0_copy(n):
        row, col_at, plane, _ = w0_place(n)
        return remote(
            stage.at[row, pl.ds(pl.multiple_of(col_at * RP, RP), RP), :],
            wb.at[y, col_at, c, half, z],
            w0s.at[n], w0r.at[half, z], ((y * X + col_at) * 2 + c, plane),
        )

    def w0_send(n, carry):
        row, col_at, plane, own = w0_place(n)

        @pl.when(own)
        def _():
            pltpu.make_async_copy(
                stage.at[row, pl.ds(pl.multiple_of(col_at * RP, RP), RP), :],
                wb.at[y, col_at, c, half, z], w0r.at[half, z],
            ).start()

        @pl.when(jnp.logical_not(own))
        def _():
            w0_copy(n).start()

        return carry

    def w0_pass():
        wq_got[0].wait()
        for got in wq_got[1:]:
            got.wait_recv()
        lax.fori_loop(0, R, w0_send, 0)

    core_copies = [
        remote(t0, t0p, cs.at[0], cr.at[0], mate),
        remote(d0, d0p, cs.at[1], cr.at[1], mate),
    ]
    for cp in core_copies:
        cp.start()

    for cp in loads[2 * HL:]:
        cp.wait()
    causal = (
        lax.broadcasted_iota(jnp.int32, (BLOCK, BLOCK), 0) >= lax.broadcasted_iota(jnp.int32, (BLOCK, BLOCK), 1)
    )

    def inside(h):
        for b in range(NB):
            rows = slice(b * BLOCK, (b + 1) * BLOCK)
            qq = qb[h, rows, :]
            score = lax.dot_general(
                qq, kb[h, rows, :], (((1,), (1,)), ((), ())), preferred_element_type=F32
            )
            gap = col[h, :, b * 16 + 8:b * 16 + 9] - wrows[pl.ds(b * HL + h, 1), :]
            decay = jnp.where(causal, jnp.exp(jnp.where(causal, gap, 0.0)), 0.0)
            lhs = [(col[h, :, b * 16:b * 16 + 1] * decay * score).astype(BF)]
            rhs = [vb[h, rows, :]]
            qf = qq.astype(F32)
            if b & 1:
                lhs.append((qf * col[h, :, b * 16 + 1:b * 16 + 2]).astype(BF))
                rhs.append(lst[h, b - 1])
            if b & 2:
                lhs.append((qf * col[h, :, b * 16 + 2:b * 16 + 3]).astype(BF))
                rhs.append(lst[h, 1])
            mix[h, rows, :] = jnp.dot(
                jnp.concatenate(lhs, axis=1), jnp.concatenate(rhs, axis=0), preferred_element_type=F32
            )

    for cp in core_copies:
        cp.wait_recv()
    fall[0] = jnp.exp(jnp.where(c == 0, d0[...], d0p[...]))
    fall[1] = jnp.exp(jnp.where(c == 0, d0p[...], d0[...]))
    xd[x] = d0[...] + d0p[...]

    def spread(bufs, at, size, ssem, rsem, dev_of, n):
        copies = []
        state, decays = bufs
        for s in range(1, size):
            src = lax.rem(at + size - s, size)
            pieces = [(state.at[at, n], state.at[src, n], n)]
            if n == 0:
                pieces.append((decays.at[at], decays.at[src], 2))
            for mine, theirs, i in pieces:
                cp = remote(mine, mine, ssem.at[s - 1, i], rsem.at[s - 1, i], (dev_of(s), z))
                cp.start()
                copies.append((cp, remote(theirs, theirs, ssem.at[s - 1, i], rsem.at[s - 1, i], (dev_of(s), z))))
        return copies

    x_copies = []
    for n in range(2):
        h = 2 * c + n
        sec = fall[1, pl.ds(h, 1), :]
        mine = t0[h].astype(F32) * jnp.where(c == 0, sec, 1.0)
        other = t0p[h].astype(F32) * jnp.where(c == 0, 1.0, sec)
        xb[x, n] = (mine + other).astype(BF)
        x_copies.append(spread((xb, xd), x, X, xs, xr, at_x, n))
    for h in range(HL):
        rb[h, 0] = jnp.where(c == 1, t0p[h].astype(F32), 0.0).astype(BF)

    inside(0)
    inside(1)
    w0_pass()

    def weighted(buf, dec, n, at, size, before, last):
        h = 2 * c + n
        d = [dec[i, pl.ds(h, 1), :] for i in range(size)]
        ends, total = [], jnp.zeros_like(d[0])
        start = jnp.zeros_like(d[0])
        for i in range(size):
            start = start + jnp.where(i < at, d[i], 0.0)
            total = total + d[i]
            ends.append(total)
        f = [buf[i, n].astype(F32) for i in range(size)]
        near = [jnp.exp(jnp.minimum(start - ends[i], 0.0) + before) for i in range(size)]
        levels = []
        for bit in range(size.bit_length() - 1):
            top = (at >> bit) << bit
            low = top - (1 << bit)
            on = ((at >> bit) & 1) == 1
            part = jnp.zeros((HD, HD), F32)
            for i in range(size):
                take = jnp.logical_and(on, jnp.logical_and(i >= low, i < top))
                part = part + jnp.where(take, near[i], 0.0) * f[i]
            levels.append(part)
        if last:
            return levels
        whole = jnp.zeros((HD, HD), F32)
        for i in range(size):
            whole = whole + jnp.exp(total - ends[i]) * f[i]
        return levels, whole, start

    def keep(n, slot, value):
        h = 2 * c + n
        lower = fall[0, pl.ds(h, 1), :]
        rb[h, 1 + slot] = (value * jnp.where(c == 1, lower, 1.0)).astype(BF)
        rs[n, slot] = (value * jnp.where(c == 0, lower, 1.0)).astype(BF)

    offsets, y_copies = [], []
    for n in range(2):
        for cp, got in x_copies[n]:
            got.wait_recv()
        if n == 0:
            yd[y] = sum(xd[i] for i in range(X))
        levels, whole, start = weighted(xb, xd, n, x, X, 0.0, False)
        yb[y, n] = whole.astype(BF)
        y_copies.append(spread((yb, yd), y, Y, ys, yr, at_y, n))
        offsets.append(start)
        for bit in range(xbits):
            keep(n, bit, levels[bit])

    inside(2)
    inside(3)

    def w0_wait(n, carry):
        a, b = n // Z, lax.rem(n, Z)
        pltpu.make_async_copy(w_ref.at[pl.ds(0, RP), :], wb.at[y, x, c, a, b], w0r.at[a, b]).wait()
        return carry

    w1 = []

    def w1_pass():
        lax.fori_loop(0, 2 * Z, w0_wait, 0)
        for s in range(1, X):
            piece, dev = wb.at[y, x, c, 0], (at_x(s), z)
            cp = remote(piece, piece, w1s.at[0, s - 1], w1r.at[0, s - 1], dev)
            cp.start()
            there = wb.at[y, lax.rem(x + X - s, X), c, 0]
            w1.append((cp, remote(there, there, w1s.at[0, s - 1], w1r.at[0, s - 1], dev)))
        for s in range(1, Y):
            piece, dev = wb.at[y, x, c, 1], (at_y(s), z)
            cp = remote(piece, piece, w1s.at[1, s - 1], w1r.at[1, s - 1], dev)
            cp.start()
            there = wb.at[lax.rem(y + Y - s, Y), x, c, 1]
            w1.append((cp, remote(there, there, w1s.at[1, s - 1], w1r.at[1, s - 1], dev)))

    H2 = Z // 2

    def travels(way, d, n):
        return d < H2 - 1 or (n < 2) == (way == 0)

    def ring(way, d, n):
        origin = lax.rem(z + (Z - d if way == 0 else d), Z)
        chunk = ab.at[origin, lax.rem(2 * c + n, HL)]
        dev = (me, right if way == 0 else left)
        return remote(chunk, chunk, rings.at[way, d, n], ringr.at[way, d, n], dev)

    def ring_got(way, d, n):
        origin = lax.rem(z + (Z - d - 1 if way == 0 else d + 1), Z)
        chunk = ab.at[origin, lax.rem(2 * c + n, HL)]
        dev = (me, right if way == 0 else left)
        return remote(chunk, chunk, rings.at[way, d, n], ringr.at[way, d, n], dev)

    def finish(h):
        for b in range(NB):
            rows = slice(b * BLOCK, (b + 1) * BLOCK)
            qf = qb[h, rows, :].astype(F32)
            lhs = jnp.concatenate(
                [(qf * col[h, :, b * 16 + 3 + n:b * 16 + 4 + n]).astype(BF) for n in range(NR)], axis=1
            )
            total = mix[h, rows, :] + jnp.dot(lhs, rb[h].reshape(NR * HD, HD), preferred_element_type=F32)
            mean = jnp.mean(total * total, axis=-1, keepdims=True)
            ab[z, h, rows, :] = (total * lax.rsqrt(mean + 1e-06)).astype(BF)

    def state_copy(n, h):
        return remote(rs.at[n], rb.at[h + n, pl.ds(1, NR - 1)], rss.at[n], rsr.at[n], mate)

    for n in range(HL):
        if n < 2:
            for cp, got in y_copies[n]:
                got.wait_recv()
            levels = weighted(yb, yd, n, y, Y, offsets[n], True)
            for bit in range(ybits):
                keep(n, xbits + bit, levels[bit])
            state_copy(n, 2 * c).start()
        else:
            state_copy(n - 2, 2 - 2 * c).wait_recv()
        finish(lax.rem(2 * c + n, HL))
        for way in range(2):
            if travels(way, 0, n):
                ring(way, 0, n).start()
    w1_pass()

    w2 = {}
    wc = []

    def block(axis, at, part, core):
        if axis == 0:
            return wb.at[at, :, core, 0] if part is None else wb.at[at, pl.ds(part * (X // 2), X // 2), core, 0]
        return wb.at[:, at, core, 1] if part is None else wb.at[pl.ds(part * (Y // 2), Y // 2), at, core, 1]

    def across(axis, at, part):
        n = len(wc)
        cp = remote(block(axis, at, part, c), block(axis, at, part, c), wcs.at[n], wcr.at[n], mate)
        cp.start()
        other = block(axis, at, part, 1 - c)
        wc.append((cp, remote(other, other, wcs.at[n], wcr.at[n], mate)))

    def near(axis, s):
        size, at = (Y, y) if axis == 0 else (X, x)
        return lax.rem(at + s + size, size)

    def w2_copy(axis, way, k):
        sign = 1 - 2 * way
        part = way if k != 1 else 1 - way
        dev = (at_y(sign % Y) if axis == 0 else at_x(sign % X), z)
        sems = (w2s.at[axis, way, k], w2r.at[axis, way, k])
        mine = block(axis, near(axis, 0 if k < 2 else -sign), part, c)
        at = near(axis, -sign if k < 2 else -2 * sign)
        theirs = block(axis, at, part, c)
        cp = remote(mine, mine, *sems, dev)
        cp.start()
        w2[axis, way, k] = (cp, remote(theirs, theirs, *sems, dev), at, part)

    def w2_pass():
        for cp, got in w1:
            got.wait_recv()
        for k in range(2):
            for axis in range(2):
                for way in range(2):
                    w2_copy(axis, way, k)
        across(0, y, None)
        across(1, x, None)

    def w3_pass(k):
        for axis in range(2):
            for way in range(2):
                _, got, at, part = w2[axis, way, k]
                got.wait_recv()
                if k == 0:
                    w2_copy(axis, way, 2)
                across(axis, at, part)

    def project(origins, first, last=False):
        def tile(u, carry):
            lhs = jnp.concatenate([ab[origin, h] for origin in origins for h in range(HL)], axis=1)
            rhs = jnp.concatenate(
                [wb[:, :, lax.rem(u, 2), u // 2, origin].reshape(TOK, COLS) for origin in origins], axis=0
            )
            part = jnp.dot(lhs, rhs, preferred_element_type=F32)
            if not first:
                part = part + acc[u]
            if last:
                ob[u] = part.astype(BF)
                out_copy(u).start()
            else:
                acc[u] = part
            return carry

        lax.fori_loop(0, 4, tile, 0)

    def out_copy(u):
        return pltpu.make_async_copy(ob.at[u], out_ref.at[:, pl.ds(pl.multiple_of(u * COLS, COLS), COLS)], out_sem.at[u])

    waiting = [[z]]
    begun = False
    for d in range(H2):
        for n in range(HL):
            for way in range(2):
                if travels(way, d, n):
                    ring_got(way, d, n).wait_recv()
                    if d + 1 < H2 and travels(way, d + 1, n):
                        ring(way, d + 1, n).start()
            slot = d * HL + n
            if slot == W2_SLOT:
                w2_pass()
            for k in range(3):
                if slot == W3_SLOTS[k]:
                    w3_pass(k)
            if slot == W3_SLOTS[2] + 1:
                for _, got in wc:
                    got.wait_recv()
            if slot > W3_SLOTS[2] and waiting:
                project(waiting.pop(0), not begun)
                begun = True
        if d + 1 < H2:
            waiting.append([lax.rem(z + Z - d - 1, Z), lax.rem(z + d + 1, Z)])
    while waiting:
        project(waiting.pop(0), not begun)
        begun = True
    project([lax.rem(z + H2, Z)], False, True)

    def w0_sent(n, carry):
        @pl.when(jnp.logical_not(w0_place(n)[3]))
        def _():
            w0_copy(n).wait_send()

        return carry

    lax.fori_loop(0, R, w0_sent, 0)
    for cp in core_copies + wq[1:]:
        cp.wait_send()
    for n in range(2):
        state_copy(n, 2 * c).wait_send()
    for cp, _ in x_copies[0] + x_copies[1] + y_copies[0] + y_copies[1] + w1 + wc + [(cp, 0) for cp, _, _, _ in w2.values()]:
        cp.wait_send()
    for way in range(2):
        for d in range(H2):
            for n in range(HL):
                if travels(way, d, n):
                    ring(way, d, n).wait_send()
    for u in range(4):
        out_copy(u).wait()


def local(X, Y, Z, queries, keys, values, log_decay, level_pick, level_table, out_weight):
    R = X * Y
    NR = 1 + (X.bit_length() - 1) + (Y.bit_length() - 1)
    H2 = Z // 2
    anyspace = pl.BlockSpec(memory_space=pl.ANY)
    dma = pltpu.SemaphoreType.DMA
    heads = (HL, TOK, HD)
    state = (HD, HD)
    scratch = [
        pltpu.VMEM((HL, TOK), F32), pltpu.VMEM((HL, TOK), jnp.int32), pltpu.VMEM(level_table.shape, F32),
        pltpu.VMEM(heads, BF), pltpu.VMEM(heads, BF), pltpu.VMEM(heads, BF),
        pltpu.VMEM((NB * HL, BLOCK), jnp.int32), pltpu.VMEM((NB * HL, BLOCK), F32), pltpu.VMEM((NB * HL, BLOCK), F32),
        pltpu.VMEM((HL, BLOCK, BLOCK), F32),
        pltpu.VMEM(heads, F32),
        pltpu.VMEM((HL, 3) + state, BF),
        pltpu.VMEM((Y, TOK // Y, COLS), BF),
        pltpu.VMEM((HL,) + state, BF), pltpu.VMEM((HL,) + state, BF),
        pltpu.VMEM((8, BLOCK), F32), pltpu.VMEM((8, BLOCK), F32), pltpu.VMEM((2, 8, BLOCK), F32),
        pltpu.VMEM((X, 2) + state, BF), pltpu.VMEM((X, 8, BLOCK), F32),
        pltpu.VMEM((Y, 2) + state, BF), pltpu.VMEM((Y, 8, BLOCK), F32),
        pltpu.VMEM((2, NR - 1) + state, BF), pltpu.VMEM((HL, NR) + state, BF),
        pltpu.VMEM((Z,) + heads, BF),
        pltpu.VMEM((Y, X, 2, 2, Z, TOK // R, COLS), BF),
        pltpu.VMEM((4, TOK, COLS), F32), pltpu.VMEM((4, TOK, COLS), BF),
        dma((4, HL)), dma((4,)),
        dma((Y,)), dma((Y,)),
        dma((R,)), dma((2, Z)),
        dma((2, max(X, Y))), dma((2, max(X, Y))),
        dma((2, 2, 3)), dma((2, 2, 3)),
        dma((14,)), dma((14,)),
        dma((2,)), dma((2,)),
        dma((X, 3)), dma((X, 3)),
        dma((Y, 3)), dma((Y, 3)),
        dma((2,)), dma((2,)),
        dma((2, H2, HL)), dma((2, H2, HL)),
    ]
    return pl.pallas_call(
        functools.partial(kernel, X, Y, Z),
        out_shape=jax.ShapeDtypeStruct((TOK, 4 * COLS), BF),
        in_specs=[anyspace] * 7,
        out_specs=anyspace,
        scratch_shapes=scratch,
        cost_estimate=pl.CostEstimate(flops=5_000_000_000, bytes_accessed=4_000_000, transcendentals=1_000_000),
        compiler_params=pltpu.CompilerParams(
            collective_id=0, has_side_effects=True, vmem_limit_bytes=61 * 1024 * 1024
        ),
    )(queries, keys, values, log_decay, level_pick, level_table, out_weight)


def solution(mesh):
    nctx, Z = mesh.shape["ctx"], mesh.shape["head"]
    chips = nctx // 2
    X = 1 << int(math.log2(chips)) // 2
    Y = chips // X
    in_specs = (
        P("ctx", "head"),
        P("ctx", "head"),
        P("ctx", "head"),
        P("head", "ctx"),
        P("head", "ctx"),
        P("head", None, None),
        P("head", "ctx"),
    )
    return jax.shard_map(
        functools.partial(local, X, Y, Z), mesh=mesh, in_specs=in_specs, out_specs=P("ctx", "head"), check_vma=False
    )
```

```python
import functools
import math

import jax
import jax.numpy as jnp
from jax import lax
from jax.experimental import pallas as pl
from jax.experimental.pallas import tpu as pltpu
from jax.sharding import PartitionSpec as P

HD = 128
BLOCK = 128
HL = 4
TOK = 512
NB = TOK // BLOCK
COLS = 256
W2_SLOT, W3_SLOTS = 2, (5, 7, 9)
MESH = pl.DeviceIdType.MESH
BF = jnp.bfloat16
F32 = jnp.float32


def kernel(
    X, Y, Z,
    q_ref, k_ref, v_ref, ld_hbm, pick_hbm, table_hbm, w_ref, out_ref,
    ld_ref, pick_ref, table_ref,
    qb, kb, vb, picks, wrows, bdrows, col, kcol, mix, lst, stage, t0, t0p, d0, d0p, fall, xb, xd, yb, yd, rs, rb, ab, wb, acc, ob,
    in_sem, out_sem, wqs, wqr, w0s, w0r, w1s, w1r, w2s, w2r, wcs, wcr, cs, cr, xs, xr, ys, yr, rss, rsr, rings, ringr, relay_sem,
):
    R = X * Y
    RP = TOK // R
    xbits = X.bit_length() - 1
    ybits = Y.bit_length() - 1
    NR = 1 + xbits + ybits
    H2 = Z // 2
    me = lax.axis_index("ctx")
    z = lax.axis_index("head")
    c = lax.rem(me, 2)
    chip = me // 2
    x = lax.rem(chip, X)
    y = chip // X
    half = lax.rem(x, 2)
    mate = (me + 1 - 2 * c, z)
    right = lax.rem(z + 1, Z)
    left = lax.rem(z + Z - 1, Z)

    def at_x(step):
        return (y * X + lax.rem(x + step, X)) * 2 + c

    def at_y(step):
        return (lax.rem(y + step, Y) * X + x) * 2 + c

    def remote(src, dst, ssem, rsem, dev):
        return pltpu.make_async_remote_copy(
            src_ref=src, dst_ref=dst, send_sem=ssem, recv_sem=rsem, device_id=dev, device_id_type=MESH
        )

    barrier = pltpu.get_barrier_semaphore()

    def greet(ctx, head):
        pl.semaphore_signal(barrier, inc=1, device_id=(ctx, head), device_id_type=MESH)

    greet(mate[0], z)
    for s in range(1, X):
        greet(at_x(s), z)
    for s in range(1, Y):
        greet(at_y(s), z)
    greet(me, right)
    greet(me, left)


    small = [
        pltpu.make_async_copy(src, dst, in_sem.at[3, n])
        for n, (src, dst) in enumerate(((ld_hbm, ld_ref), (pick_hbm, pick_ref), (table_hbm, table_ref)))
    ]
    for cp in small:
        cp.start()
    loads = []
    for n, (src, dst) in enumerate(((k_ref, kb), (v_ref, vb), (q_ref, qb))):
        for h in range(HL):
            cp = pltpu.make_async_copy(src.at[:, h * HD:(h + 1) * HD], dst.at[h], in_sem.at[n, h])
            cp.start()
            loads.append(cp)

    for cp in small:
        cp.wait()

    for b in range(NB):
        wrows[b * HL:(b + 1) * HL, :] = ld_ref[:, b * BLOCK:(b + 1) * BLOCK]
        picks[b * HL:(b + 1) * HL, :] = pick_ref[:, b * BLOCK:(b + 1) * BLOCK]
    run = wrows[...]
    lane = lax.broadcasted_iota(jnp.int32, run.shape, 1)
    step = 1
    while step < BLOCK:
        run = run + jnp.where(lane >= step, pltpu.roll(run, step, 1), 0.0)
        step *= 2
    wrows[...] = run
    bdrows[...] = jnp.broadcast_to(run[:, BLOCK - 1:BLOCK], run.shape)
    scale = jnp.exp(bdrows[...] - run)
    kcol[...] = jnp.concatenate([scale, jnp.zeros((BLOCK - NB * HL, BLOCK), F32)], axis=0).T
    d0[...] = jnp.zeros_like(d0)
    d0[0:HL, :] = sum(bdrows[b * HL:(b + 1) * HL, :] for b in range(NB))

    for cp in loads[:2 * HL]:
        cp.wait()

    for h in range(HL):
        s = []
        for b in range(NB):
            kk = kb[h, b * BLOCK:(b + 1) * BLOCK, :].astype(F32)
            kk = (kk * kcol[:, b * HL + h:b * HL + h + 1]).astype(BF)
            s.append(lax.dot_general(
                kk, vb[h, b * BLOCK:(b + 1) * BLOCK, :], (((0,), (0,)), ((), ())), preferred_element_type=F32
            ))
        e = [jnp.exp(bdrows[b * HL + h:b * HL + h + 1, :]) for b in range(NB)]
        pair = e[1] * s[0] + s[1]
        lst[h, 0] = s[0].astype(BF)
        lst[h, 1] = pair.astype(BF)
        lst[h, 2] = s[2].astype(BF)
        t0[h] = (e[3] * (e[2] * pair + s[2]) + s[3]).astype(BF)

    pl.semaphore_wait(barrier, 1 + (X - 1) + (Y - 1) + 2)

    core_copies = [
        remote(t0, t0p, cs.at[0], cr.at[0], mate),
        remote(d0, d0p, cs.at[1], cr.at[1], mate),
    ]
    for cp in core_copies:
        cp.start()

    def relay(turn):
        if turn > 0:
            pl.semaphore_wait(relay_sem.at[turn - 1], 2 if turn < H2 else X - 1)
        if turn < H2 - 1:
            for head in (left, right):
                pl.semaphore_signal(relay_sem.at[turn], inc=1, device_id=(me, head), device_id_type=MESH)
        elif turn == H2 - 1:
            for s in range(1, X):
                pl.semaphore_signal(relay_sem.at[turn], inc=1, device_id=(at_x(s), z), device_id_type=MESH)

    relay(0)

    def wq_move(to, start):
        def both(way):
            src = w_ref.at[to] if way == 0 else w_ref.at[:, to]
            if start == 0:
                return pltpu.make_async_copy(src, stage.at[y], wqr.at[0])
            return remote(src, stage.at[y], wqs.at[start], wqr.at[start], (at_y(start), z))

        for way in range(2):
            @pl.when(half == way)
            def _():
                both(way).start()

    def wq_done(start):
        src = lax.rem(y + Y - start, Y)
        if start == 0:
            return pltpu.make_async_copy(w_ref.at[0], stage.at[src], wqr.at[0])
        return remote(w_ref.at[0], stage.at[src], wqs.at[start], wqr.at[start], (at_y(start), z))

    def w0_place(n):
        row, col_at = lax.rem(n // X + y, Y), lax.rem(n + x, X)
        plane = 2 * row + x // 2
        return row, col_at, plane, jnp.logical_and(plane == z, col_at == x)

    def w0_copy(n):
        row, col_at, plane, _ = w0_place(n)
        return remote(
            stage.at[row, col_at],
            wb.at[y, col_at, c, half, z],
            w0s.at[n], w0r.at[half, z], ((y * X + col_at) * 2 + c, plane),
        )

    def w0_send(n, carry):
        row, col_at, plane, own = w0_place(n)

        @pl.when(own)
        def _():
            pltpu.make_async_copy(
                stage.at[row, col_at],
                wb.at[y, col_at, c, half, z], w0r.at[half, z],
            ).start()

        @pl.when(jnp.logical_not(own))
        def _():
            w0_copy(n).start()

        return carry

    def w0_pass():
        wq_done(0).wait()
        for step in range(1, Y):
            wq_done(step).wait_recv()
        lax.fori_loop(0, R, w0_send, 0)

    for step in range(Y):
        wq_move(lax.rem(y + step, Y), step)

    sub = lax.broadcasted_iota(jnp.int32, (8, BLOCK), 0)

    def prepare(h, carry):
        tab = table_ref[h]
        bd = [bdrows[pl.ds(b * HL + h, 1), :] for b in range(NB)]
        start = jnp.zeros_like(bd[0])
        rows = []
        for b in range(NB):
            pk = jnp.broadcast_to(picks[pl.ds(b * HL + h, 1), :], (8, BLOCK))
            lw = jnp.zeros((8, BLOCK), F32)
            for n in range(16):
                lw = jnp.where(pk == n, tab[:, n:n + 1], lw)
            wr = wrows[pl.ds(b * HL + h, 1), :]
            upper = jnp.where(sub >= 3, start, 0.0)
            if b == 3:
                upper = jnp.where(sub == 2, bd[2], upper)
            rows.append(lw * jnp.where(sub == 0, 1.0, jnp.exp(wr + upper)))
            rows.append(jnp.where(sub == 0, wr, 0.0))
            start = start + bd[b]
        rows.append(jnp.zeros((BLOCK - 16 * NB, BLOCK), F32))
        col[h] = jnp.concatenate(rows, axis=0).T
        return carry

    lax.fori_loop(0, HL, prepare, 0)

    for cp in loads[2 * HL:]:
        cp.wait()
    causal = (
        lax.broadcasted_iota(jnp.int32, (BLOCK, BLOCK), 0) >= lax.broadcasted_iota(jnp.int32, (BLOCK, BLOCK), 1)
    )

    def inside(h):
        for b in range(NB):
            rows = slice(b * BLOCK, (b + 1) * BLOCK)
            qq = qb[h, rows, :]
            score = lax.dot_general(
                qq, kb[h, rows, :], (((1,), (1,)), ((), ())), preferred_element_type=F32
            )
            gap = col[h, :, b * 16 + 8:b * 16 + 9] - wrows[pl.ds(b * HL + h, 1), :]
            decay = jnp.where(causal, jnp.exp(jnp.where(causal, gap, 0.0)), 0.0)
            lhs = [(col[h, :, b * 16:b * 16 + 1] * decay * score).astype(BF)]
            rhs = [vb[h, rows, :]]
            qf = qq.astype(F32)
            if b & 1:
                lhs.append((qf * col[h, :, b * 16 + 1:b * 16 + 2]).astype(BF))
                rhs.append(lst[h, b - 1])
            if b & 2:
                lhs.append((qf * col[h, :, b * 16 + 2:b * 16 + 3]).astype(BF))
                rhs.append(lst[h, 1])
            mix[h, rows, :] = jnp.dot(
                jnp.concatenate(lhs, axis=1), jnp.concatenate(rhs, axis=0), preferred_element_type=F32
            )

    for cp in core_copies:
        cp.wait_recv()
    fall[0] = jnp.exp(jnp.where(c == 0, d0[...], d0p[...]))
    fall[1] = jnp.exp(jnp.where(c == 0, d0p[...], d0[...]))
    xd[x] = d0[...] + d0p[...]

    def spread(bufs, at, size, ssem, rsem, dev_of, n):
        copies = []
        state, decays = bufs
        for s in range(1, size):
            src = lax.rem(at + size - s, size)
            pieces = [(state.at[at, n], state.at[src, n], n)]
            if n == 0:
                pieces.append((decays.at[at], decays.at[src], 2))
            for mine, theirs, i in pieces:
                cp = remote(mine, mine, ssem.at[s - 1, i], rsem.at[s - 1, i], (dev_of(s), z))
                cp.start()
                copies.append((cp, remote(theirs, theirs, ssem.at[s - 1, i], rsem.at[s - 1, i], (dev_of(s), z))))
        return copies

    relay(1)
    x_copies = []
    for n in range(2):
        h = 2 * c + n
        sec = fall[1, pl.ds(h, 1), :]
        mine = t0[h].astype(F32) * jnp.where(c == 0, sec, 1.0)
        other = t0p[h].astype(F32) * jnp.where(c == 0, 1.0, sec)
        xb[x, n] = (mine + other).astype(BF)
        x_copies.append(spread((xb, xd), x, X, xs, xr, at_x, n))
    for h in range(HL):
        rb[h, 0] = jnp.where(c == 1, t0p[h].astype(F32), 0.0).astype(BF)

    relay(2)
    inside(0)
    relay(H2 - 1)
    inside(1)
    relay(H2)
    w0_pass()

    def weighted(buf, dec, n, at, size, before, last):
        h = 2 * c + n
        d = [dec[i, pl.ds(h, 1), :] for i in range(size)]
        ends, total = [], jnp.zeros_like(d[0])
        start = jnp.zeros_like(d[0])
        for i in range(size):
            start = start + jnp.where(i < at, d[i], 0.0)
            total = total + d[i]
            ends.append(total)
        f = [buf[i, n].astype(F32) for i in range(size)]
        near = [jnp.exp(jnp.minimum(start - ends[i], 0.0) + before) for i in range(size)]
        levels = []
        for bit in range(size.bit_length() - 1):
            top = (at >> bit) << bit
            low = top - (1 << bit)
            on = ((at >> bit) & 1) == 1
            part = jnp.zeros((HD, HD), F32)
            for i in range(size):
                take = jnp.logical_and(on, jnp.logical_and(i >= low, i < top))
                part = part + jnp.where(take, near[i], 0.0) * f[i]
            levels.append(part)
        if last:
            return levels
        whole = jnp.zeros((HD, HD), F32)
        for i in range(size):
            whole = whole + jnp.exp(total - ends[i]) * f[i]
        return levels, whole, start

    def keep(n, slot, value):
        h = 2 * c + n
        lower = fall[0, pl.ds(h, 1), :]
        rb[h, 1 + slot] = (value * jnp.where(c == 1, lower, 1.0)).astype(BF)
        rs[n, slot] = (value * jnp.where(c == 0, lower, 1.0)).astype(BF)

    offsets, y_copies = [], []
    for n in range(2):
        for cp, got in x_copies[n]:
            got.wait_recv()
        if n == 0:
            yd[y] = sum(xd[i] for i in range(X))
        levels, whole, start = weighted(xb, xd, n, x, X, 0.0, False)
        yb[y, n] = whole.astype(BF)
        y_copies.append(spread((yb, yd), y, Y, ys, yr, at_y, n))
        offsets.append(start)
        for bit in range(xbits):
            keep(n, bit, levels[bit])

    inside(2)
    inside(3)

    def w0_wait(n, carry):
        a, b = n // Z, lax.rem(n, Z)
        pltpu.make_async_copy(w_ref.at[0, 0], wb.at[y, x, c, a, b], w0r.at[a, b]).wait()
        return carry

    w1 = []

    def w1_pass():
        lax.fori_loop(0, 2 * Z, w0_wait, 0)
        for s in range(1, X):
            piece, dev = wb.at[y, x, c, 0], (at_x(s), z)
            cp = remote(piece, piece, w1s.at[0, s - 1], w1r.at[0, s - 1], dev)
            cp.start()
            there = wb.at[y, lax.rem(x + X - s, X), c, 0]
            w1.append((cp, remote(there, there, w1s.at[0, s - 1], w1r.at[0, s - 1], dev)))
        for s in range(1, Y):
            piece, dev = wb.at[y, x, c, 1], (at_y(s), z)
            cp = remote(piece, piece, w1s.at[1, s - 1], w1r.at[1, s - 1], dev)
            cp.start()
            there = wb.at[lax.rem(y + Y - s, Y), x, c, 1]
            w1.append((cp, remote(there, there, w1s.at[1, s - 1], w1r.at[1, s - 1], dev)))

    def travels(way, d, n):
        return d < H2 - 1 or (n < 2) == (way == 0)

    def ring(way, d, n):
        origin = lax.rem(z + (Z - d if way == 0 else d), Z)
        chunk = ab.at[origin, lax.rem(2 * c + n, HL)]
        dev = (me, right if way == 0 else left)
        return remote(chunk, chunk, rings.at[way, d, n], ringr.at[way, d, n], dev)

    def ring_got(way, d, n):
        origin = lax.rem(z + (Z - d - 1 if way == 0 else d + 1), Z)
        chunk = ab.at[origin, lax.rem(2 * c + n, HL)]
        dev = (me, right if way == 0 else left)
        return remote(chunk, chunk, rings.at[way, d, n], ringr.at[way, d, n], dev)

    def finish(h):
        for b in range(NB):
            rows = slice(b * BLOCK, (b + 1) * BLOCK)
            qf = qb[h, rows, :].astype(F32)
            lhs = jnp.concatenate(
                [(qf * col[h, :, b * 16 + 3 + n:b * 16 + 4 + n]).astype(BF) for n in range(NR)], axis=1
            )
            total = mix[h, rows, :] + jnp.dot(lhs, rb[h].reshape(NR * HD, HD), preferred_element_type=F32)
            mean = jnp.mean(total * total, axis=-1, keepdims=True)
            ab[z, h, rows, :] = (total * lax.rsqrt(mean + 1e-06)).astype(BF)

    def state_copy(n, h):
        return remote(rs.at[n], rb.at[h + n, pl.ds(1, NR - 1)], rss.at[n], rsr.at[n], mate)

    for n in range(HL):
        if n < 2:
            for cp, got in y_copies[n]:
                got.wait_recv()
            levels = weighted(yb, yd, n, y, Y, offsets[n], True)
            for bit in range(ybits):
                keep(n, xbits + bit, levels[bit])
            state_copy(n, 2 * c).start()
        else:
            state_copy(n - 2, 2 - 2 * c).wait_recv()
        finish(lax.rem(2 * c + n, HL))
        for way in range(2):
            if travels(way, 0, n):
                ring(way, 0, n).start()
    w1_pass()

    w2 = {}
    wc = []

    def block(axis, at, part, core):
        if axis == 0:
            return wb.at[at, :, core, 0] if part is None else wb.at[at, pl.ds(part * (X // 2), X // 2), core, 0]
        return wb.at[:, at, core, 1] if part is None else wb.at[pl.ds(part * (Y // 2), Y // 2), at, core, 1]

    def across(axis, at, part):
        n = len(wc)
        cp = remote(block(axis, at, part, c), block(axis, at, part, c), wcs.at[n], wcr.at[n], mate)
        cp.start()
        other = block(axis, at, part, 1 - c)
        wc.append((cp, remote(other, other, wcs.at[n], wcr.at[n], mate)))

    def near(axis, s):
        size, at = (Y, y) if axis == 0 else (X, x)
        return lax.rem(at + s + size, size)

    def w2_copy(axis, way, k):
        sign = 1 - 2 * way
        part = way if k != 1 else 1 - way
        dev = (at_y(sign % Y) if axis == 0 else at_x(sign % X), z)
        sems = (w2s.at[axis, way, k], w2r.at[axis, way, k])
        mine = block(axis, near(axis, 0 if k < 2 else -sign), part, c)
        at = near(axis, -sign if k < 2 else -2 * sign)
        theirs = block(axis, at, part, c)
        cp = remote(mine, mine, *sems, dev)
        cp.start()
        w2[axis, way, k] = (cp, remote(theirs, theirs, *sems, dev), at, part)

    def w2_pass():
        for cp, got in w1:
            got.wait_recv()
        for k in range(2):
            for axis in range(2):
                for way in range(2):
                    w2_copy(axis, way, k)
        across(0, y, None)
        across(1, x, None)

    def w3_pass(k):
        for axis in range(2):
            for way in range(2):
                _, got, at, part = w2[axis, way, k]
                got.wait_recv()
                if k == 0:
                    w2_copy(axis, way, 2)
                across(axis, at, part)

    def project(origins, first, last=False, heads=range(HL), shifted=False):
        for part in range(2):
            pick = [h if not shifted else lax.rem((y, x)[part] + h, HL) for h in heads]

            def tile(core, carry):
                u = 2 * part + core
                lhs = jnp.concatenate([ab[origin, h] for origin in origins for h in pick], axis=1)
                rhs = jnp.concatenate([
                    (wb[h, :, core, 0, origin] if part == 0 else wb[:, h, core, 1, origin]).reshape(HD, COLS)
                    for origin in origins for h in pick
                ], axis=0)
                total = jnp.dot(lhs, rhs, preferred_element_type=F32)
                if not first:
                    total = total + acc[u]
                if last:
                    ob[u] = total.astype(BF)
                    out_copy(u).start()
                else:
                    acc[u] = total
                return carry

            lax.fori_loop(0, 2, tile, 0)

    def out_copy(u):
        return pltpu.make_async_copy(ob.at[u], out_ref.at[:, pl.ds(pl.multiple_of(u * COLS, COLS), COLS)], out_sem.at[u])

    waiting = [[z]]
    behind = []
    begun = False
    for d in range(H2 - 1):
        for n in range(HL):
            for way in range(2):
                ring_got(way, d, n).wait_recv()
                if travels(way, d + 1, n):
                    ring(way, d + 1, n).start()
            slot = d * HL + n
            if slot == W2_SLOT:
                w2_pass()
            for k in range(3):
                if slot == W3_SLOTS[k]:
                    w3_pass(k)
            if slot == W3_SLOTS[1] + 1:
                for _, got in wc[:10]:
                    got.wait_recv()
            if W3_SLOTS[1] < slot <= W3_SLOTS[2] and waiting:
                project(waiting[0], not begun, False, (0, 1, 3), True)
                begun = True
                behind += waiting.pop(0)
            if slot == W3_SLOTS[2] + 1:
                for _, got in wc[10:]:
                    got.wait_recv()
                project(behind, False, False, (2,), True)
            elif slot > W3_SLOTS[2] and waiting:
                project(waiting.pop(0), False)
        waiting.append([lax.rem(z + Z - d - 1, Z), lax.rem(z + d + 1, Z)])
    while waiting:
        project(waiting.pop(0), False)
    for n in range(2):
        ring_got(0, H2 - 1, n).wait_recv()
        ring_got(1, H2 - 1, n + 2).wait_recv()
        project([lax.rem(z + H2, Z)], False, n == 1, (n, n + 2))

    def w0_sent(n, carry):
        @pl.when(jnp.logical_not(w0_place(n)[3]))
        def _():
            w0_copy(n).wait_send()

        return carry

    lax.fori_loop(0, R, w0_sent, 0)
    for cp in core_copies:
        cp.wait_send()
    for step in range(1, Y):
        wq_done(step).wait_send()
    for n in range(2):
        state_copy(n, 2 * c).wait_send()
    for cp, _ in x_copies[0] + x_copies[1] + y_copies[0] + y_copies[1] + w1 + wc + [(cp, 0) for cp, _, _, _ in w2.values()]:
        cp.wait_send()
    for way in range(2):
        for d in range(H2):
            for n in range(HL):
                if travels(way, d, n):
                    ring(way, d, n).wait_send()
    for u in range(4):
        out_copy(u).wait()


def local(X, Y, Z, queries, keys, values, log_decay, level_pick, level_table, out_weight):
    R = X * Y
    NR = 1 + (X.bit_length() - 1) + (Y.bit_length() - 1)
    H2 = Z // 2
    anyspace = pl.BlockSpec(memory_space=pl.ANY)
    dma = pltpu.SemaphoreType.DMA
    heads = (HL, TOK, HD)
    state = (HD, HD)
    scratch = [
        pltpu.VMEM((HL, TOK), F32), pltpu.VMEM((HL, TOK), jnp.int32), pltpu.VMEM(level_table.shape, F32),
        pltpu.VMEM(heads, BF), pltpu.VMEM(heads, BF), pltpu.VMEM(heads, BF),
        pltpu.VMEM((NB * HL, BLOCK), jnp.int32), pltpu.VMEM((NB * HL, BLOCK), F32), pltpu.VMEM((NB * HL, BLOCK), F32),
        pltpu.VMEM((HL, BLOCK, BLOCK), F32), pltpu.VMEM((BLOCK, BLOCK), F32),
        pltpu.VMEM(heads, F32),
        pltpu.VMEM((HL, 3) + state, BF),
        pltpu.VMEM((Y, X, TOK // R, COLS), BF),
        pltpu.VMEM((HL,) + state, BF), pltpu.VMEM((HL,) + state, BF),
        pltpu.VMEM((8, BLOCK), F32), pltpu.VMEM((8, BLOCK), F32), pltpu.VMEM((2, 8, BLOCK), F32),
        pltpu.VMEM((X, 2) + state, BF), pltpu.VMEM((X, 8, BLOCK), F32),
        pltpu.VMEM((Y, 2) + state, BF), pltpu.VMEM((Y, 8, BLOCK), F32),
        pltpu.VMEM((2, NR - 1) + state, BF), pltpu.VMEM((HL, NR) + state, BF),
        pltpu.VMEM((Z,) + heads, BF),
        pltpu.VMEM((Y, X, 2, 2, Z, TOK // R, COLS), BF),
        pltpu.VMEM((4, TOK, COLS), F32), pltpu.VMEM((4, TOK, COLS), BF),
        dma((4, HL)), dma((4,)),
        dma((Y,)), dma((Y,)),
        dma((R,)), dma((2, Z)),
        dma((2, max(X, Y))), dma((2, max(X, Y))),
        dma((2, 2, 3)), dma((2, 2, 3)),
        dma((14,)), dma((14,)),
        dma((2,)), dma((2,)),
        dma((X, 3)), dma((X, 3)),
        dma((Y, 3)), dma((Y, 3)),
        dma((2,)), dma((2,)),
        dma((2, H2, HL)), dma((2, H2, HL)),
        pltpu.SemaphoreType.REGULAR((H2,)),
    ]
    return pl.pallas_call(
        functools.partial(kernel, X, Y, Z),
        out_shape=jax.ShapeDtypeStruct((TOK, 4 * COLS), BF),
        in_specs=[anyspace] * 7,
        out_specs=anyspace,
        scratch_shapes=scratch,
        cost_estimate=pl.CostEstimate(flops=5_000_000_000, bytes_accessed=4_000_000, transcendentals=1_000_000),
        compiler_params=pltpu.CompilerParams(
            collective_id=0, has_side_effects=True, vmem_limit_bytes=61 * 1024 * 1024
        ),
    )(queries, keys, values, log_decay, level_pick, level_table, out_weight.reshape(Y, X, TOK // R, COLS))


def solution(mesh):
    nctx, Z = mesh.shape["ctx"], mesh.shape["head"]
    chips = nctx // 2
    X = 1 << int(math.log2(chips)) // 2
    Y = chips // X
    in_specs = (
        P("ctx", "head"),
        P("ctx", "head"),
        P("ctx", "head"),
        P("head", "ctx"),
        P("head", "ctx"),
        P("head", None, None),
        P("head", "ctx"),
    )
    return jax.shard_map(
        functools.partial(local, X, Y, Z), mesh=mesh, in_specs=in_specs, out_specs=P("ctx", "head"), check_vma=False
    )
```

```python
import functools
import math

import jax
import jax.numpy as jnp
from jax import lax
from jax.experimental import pallas as pl
from jax.experimental.pallas import tpu as pltpu
from jax.sharding import PartitionSpec as P

HD = 128
BLOCK = 128
HL = 4
TOK = 512
NB = TOK // BLOCK
COLS = 256
W2_SLOT, W3_SLOTS = 1, (4, 6, 9)
MESH = pl.DeviceIdType.MESH
BF = jnp.bfloat16
F32 = jnp.float32


def kernel(
    X, Y, Z,
    q_ref, k_ref, v_ref, ld_hbm, pick_hbm, table_hbm, w_ref, out_ref,
    ld_ref, pick_ref, table_ref,
    qb, kb, vb, picks, wrows, bdrows, col, kcol, mix, lst, stage, t0, t0p, d0, d0p, fall, xb, xd, yb, yd, rs, rb, ab, wb, acc, ob,
    in_sem, out_sem, wqs, wqr, w0s, w0r, w1s, w1r, w2s, w2r, wcs, wcr, cs, cr, xs, xr, ys, yr, rss, rsr, rings, ringr, relay_sem,
):
    R = X * Y
    RP = TOK // R
    xbits = X.bit_length() - 1
    ybits = Y.bit_length() - 1
    NR = 1 + xbits + ybits
    H2 = Z // 2
    me = lax.axis_index("ctx")
    z = lax.axis_index("head")
    c = lax.rem(me, 2)
    chip = me // 2
    x = lax.rem(chip, X)
    y = chip // X
    half = lax.rem(x, 2)
    mate = (me + 1 - 2 * c, z)
    right = lax.rem(z + 1, Z)
    left = lax.rem(z + Z - 1, Z)

    def at_x(step):
        return (y * X + lax.rem(x + step, X)) * 2 + c

    def at_y(step):
        return (lax.rem(y + step, Y) * X + x) * 2 + c

    def remote(src, dst, ssem, rsem, dev):
        return pltpu.make_async_remote_copy(
            src_ref=src, dst_ref=dst, send_sem=ssem, recv_sem=rsem, device_id=dev, device_id_type=MESH
        )

    barrier = pltpu.get_barrier_semaphore()

    def greet(ctx, head):
        pl.semaphore_signal(barrier, inc=1, device_id=(ctx, head), device_id_type=MESH)

    greet(mate[0], z)
    for s in range(1, X):
        greet(at_x(s), z)
    for s in range(1, Y):
        greet(at_y(s), z)
    for s in range(1, Y):
        greet((lax.rem(y + s, Y) * X + lax.rem(x + 2, X)) * 2 + c, z)
    for s in (1, 2, Z - 2, Z - 1):
        greet(me, lax.rem(z + s, Z))


    small = [
        pltpu.make_async_copy(src, dst, in_sem.at[3, n])
        for n, (src, dst) in enumerate(((ld_hbm, ld_ref), (pick_hbm, pick_ref), (table_hbm, table_ref)))
    ]
    for cp in small:
        cp.start()
    loads = []
    for n, (src, dst) in enumerate(((k_ref, kb), (v_ref, vb), (q_ref, qb))):
        for h in range(HL):
            cp = pltpu.make_async_copy(src.at[:, h * HD:(h + 1) * HD], dst.at[h], in_sem.at[n, h])
            cp.start()
            loads.append(cp)

    for cp in small:
        cp.wait()

    for b in range(NB):
        wrows[b * HL:(b + 1) * HL, :] = ld_ref[:, b * BLOCK:(b + 1) * BLOCK]
        picks[b * HL:(b + 1) * HL, :] = pick_ref[:, b * BLOCK:(b + 1) * BLOCK]
    run = wrows[...]
    lane = lax.broadcasted_iota(jnp.int32, run.shape, 1)
    step = 1
    while step < BLOCK:
        run = run + jnp.where(lane >= step, pltpu.roll(run, step, 1), 0.0)
        step *= 2
    wrows[...] = run
    bdrows[...] = jnp.broadcast_to(run[:, BLOCK - 1:BLOCK], run.shape)
    scale = jnp.exp(bdrows[...] - run)
    kcol[...] = jnp.concatenate([scale, jnp.zeros((BLOCK - NB * HL, BLOCK), F32)], axis=0).T
    d0[...] = jnp.zeros_like(d0)
    d0[0:HL, :] = sum(bdrows[b * HL:(b + 1) * HL, :] for b in range(NB))

    for cp in loads[:2 * HL]:
        cp.wait()

    for h in range(HL):
        s = []
        for b in range(NB):
            kk = kb[h, b * BLOCK:(b + 1) * BLOCK, :].astype(F32)
            kk = (kk * kcol[:, b * HL + h:b * HL + h + 1]).astype(BF)
            s.append(lax.dot_general(
                kk, vb[h, b * BLOCK:(b + 1) * BLOCK, :], (((0,), (0,)), ((), ())), preferred_element_type=F32
            ))
        e = [jnp.exp(bdrows[b * HL + h:b * HL + h + 1, :]) for b in range(NB)]
        pair = e[1] * s[0] + s[1]
        lst[h, 0] = s[0].astype(BF)
        lst[h, 1] = pair.astype(BF)
        lst[h, 2] = s[2].astype(BF)
        t0[h] = (e[3] * (e[2] * pair + s[2]) + s[3]).astype(BF)

    pl.semaphore_wait(barrier, 1 + (X - 1) + 2 * (Y - 1) + 4)

    core_copies = [
        remote(t0, t0p, cs.at[0], cr.at[0], mate),
        remote(d0, d0p, cs.at[1], cr.at[1], mate),
    ]
    for cp in core_copies:
        cp.start()

    beside = x + 1 - 2 * lax.rem(x, 2)

    def relay(turn):
        if turn > 0:
            pl.semaphore_wait(relay_sem.at[turn - 1], 4 if turn == 1 else 1)
        if turn == 0:
            for s in (1, 2, Z - 2, Z - 1):
                pl.semaphore_signal(
                    relay_sem.at[0], inc=1, device_id=(me, lax.rem(z + s, Z)), device_id_type=MESH
                )
        elif turn == 1:
            pl.semaphore_signal(
                relay_sem.at[1], inc=1, device_id=((y * X + beside) * 2 + c, z), device_id_type=MESH
            )

    relay(0)

    far = lax.rem(x + 2, X)

    def spread_to(other, step):
        return ((lax.rem(y + step, Y) * X + (far if other else x)) * 2 + c, z)

    def wq_move(other, step):
        group = 1 - x // 2 if other else x // 2
        pair, row = pl.ds(2 * group, 2), lax.rem(y + step, Y)
        for way in range(2):
            @pl.when(half == way)
            def _():
                src = w_ref.at[row, pair] if way == 0 else w_ref.at[pair, row]
                dst = stage.at[x // 2, y]
                if not other and step == 0:
                    pltpu.make_async_copy(src, dst, wqr.at[0, 0]).start()
                else:
                    remote(src, dst, wqs.at[other, step], wqr.at[other, step], spread_to(other, step)).start()

    def wq_done(other, step):
        src, dst = w_ref.at[0, pl.ds(0, 2)], stage.at[1 - x // 2 if other else x // 2, lax.rem(y + Y - step, Y)]
        if not other and step == 0:
            return pltpu.make_async_copy(src, dst, wqr.at[0, 0])
        return remote(src, dst, wqs.at[other, step], wqr.at[other, step], spread_to(other, step))

    def w0_place(n):
        plane, low = lax.rem(n // 2 + z, Z), lax.rem(n + x, 2)
        col_at = x // 2 * 2 + low
        return plane, low, col_at, jnp.logical_and(plane == z, col_at == x)

    def w0_copy(n):
        plane, low, col_at, _ = w0_place(n)
        return remote(
            stage.at[lax.rem(plane, 2), plane // 2, low],
            wb.at[y, col_at, c, half, z],
            w0s.at[n], w0r.at[half, z], ((y * X + col_at) * 2 + c, plane),
        )

    def w0_send(n, carry):
        plane, low, col_at, own = w0_place(n)

        @pl.when(own)
        def _():
            pltpu.make_async_copy(
                stage.at[lax.rem(plane, 2), plane // 2, low],
                wb.at[y, col_at, c, half, z], w0r.at[half, z],
            ).start()

        @pl.when(jnp.logical_not(own))
        def _():
            w0_copy(n).start()

        return carry

    def w0_pass():
        for other in range(2):
            for step in range(Y):
                if other + step == 0:
                    wq_done(0, 0).wait()
                else:
                    wq_done(other, step).wait_recv()
        lax.fori_loop(0, R, w0_send, 0)

    for step in range(Y):
        wq_move(0, step)
        wq_move(1, step)

    for cp in loads[2 * HL:]:
        cp.wait()
    causal = (
        lax.broadcasted_iota(jnp.int32, (BLOCK, BLOCK), 0) >= lax.broadcasted_iota(jnp.int32, (BLOCK, BLOCK), 1)
    )

    def inside(h):
        for b in range(NB):
            rows = slice(b * BLOCK, (b + 1) * BLOCK)
            qq = qb[h, rows, :]
            score = lax.dot_general(
                qq, kb[h, rows, :], (((1,), (1,)), ((), ())), preferred_element_type=F32
            )
            gap = col[h, :, b * 16 + 8:b * 16 + 9] - wrows[pl.ds(b * HL + h, 1), :]
            decay = jnp.where(causal, jnp.exp(jnp.where(causal, gap, 0.0)), 0.0)
            lhs = [(col[h, :, b * 16:b * 16 + 1] * decay * score).astype(BF)]
            rhs = [vb[h, rows, :]]
            qf = qq.astype(F32)
            if b & 1:
                lhs.append((qf * col[h, :, b * 16 + 1:b * 16 + 2]).astype(BF))
                rhs.append(lst[h, b - 1])
            if b & 2:
                lhs.append((qf * col[h, :, b * 16 + 2:b * 16 + 3]).astype(BF))
                rhs.append(lst[h, 1])
            mix[h, rows, :] = jnp.dot(
                jnp.concatenate(lhs, axis=1), jnp.concatenate(rhs, axis=0), preferred_element_type=F32
            )

    for cp in core_copies:
        cp.wait_recv()
    fall[0] = jnp.exp(jnp.where(c == 0, d0[...], d0p[...]))
    fall[1] = jnp.exp(jnp.where(c == 0, d0p[...], d0[...]))
    xd[x] = d0[...] + d0p[...]

    def spread(bufs, at, size, ssem, rsem, dev_of, n):
        copies = []
        state, decays = bufs
        for s in range(1, size):
            src = lax.rem(at + size - s, size)
            pieces = [(state.at[at, n], state.at[src, n], n)]
            if n == 0:
                pieces.append((decays.at[at], decays.at[src], 2))
            for mine, theirs, i in pieces:
                cp = remote(mine, mine, ssem.at[s - 1, i], rsem.at[s - 1, i], (dev_of(s), z))
                cp.start()
                copies.append((cp, remote(theirs, theirs, ssem.at[s - 1, i], rsem.at[s - 1, i], (dev_of(s), z))))
        return copies

    x_copies = []
    for n in range(2):
        h = 2 * c + n
        sec = fall[1, pl.ds(h, 1), :]
        mine = t0[h].astype(F32) * jnp.where(c == 0, sec, 1.0)
        other = t0p[h].astype(F32) * jnp.where(c == 0, 1.0, sec)
        xb[x, n] = (mine + other).astype(BF)
        x_copies.append(spread((xb, xd), x, X, xs, xr, at_x, n))
    relay(1)
    sub = lax.broadcasted_iota(jnp.int32, (8, BLOCK), 0)

    def prepare(h, carry):
        tab = table_ref[h]
        bd = [bdrows[pl.ds(b * HL + h, 1), :] for b in range(NB)]
        start = jnp.zeros_like(bd[0])
        rows = []
        for b in range(NB):
            pk = jnp.broadcast_to(picks[pl.ds(b * HL + h, 1), :], (8, BLOCK))
            lw = jnp.zeros((8, BLOCK), F32)
            for n in range(16):
                lw = jnp.where(pk == n, tab[:, n:n + 1], lw)
            wr = wrows[pl.ds(b * HL + h, 1), :]
            upper = jnp.where(sub >= 3, start, 0.0)
            if b == 3:
                upper = jnp.where(sub == 2, bd[2], upper)
            rows.append(lw * jnp.where(sub == 0, 1.0, jnp.exp(wr + upper)))
            rows.append(jnp.where(sub == 0, wr, 0.0))
            start = start + bd[b]
        rows.append(jnp.zeros((BLOCK - 16 * NB, BLOCK), F32))
        col[h] = jnp.concatenate(rows, axis=0).T
        return carry

    lax.fori_loop(0, HL, prepare, 0)

    for h in range(HL):
        rb[h, 0] = jnp.where(c == 1, t0p[h].astype(F32), 0.0).astype(BF)

    inside(0)
    relay(2)
    w0_pass()
    inside(1)

    def weighted(buf, dec, n, at, size, before, last):
        h = 2 * c + n
        d = [dec[i, pl.ds(h, 1), :] for i in range(size)]
        ends, total = [], jnp.zeros_like(d[0])
        start = jnp.zeros_like(d[0])
        for i in range(size):
            start = start + jnp.where(i < at, d[i], 0.0)
            total = total + d[i]
            ends.append(total)
        f = [buf[i, n].astype(F32) for i in range(size)]
        near = [jnp.exp(jnp.minimum(start - ends[i], 0.0) + before) for i in range(size)]
        levels = []
        for bit in range(size.bit_length() - 1):
            top = (at >> bit) << bit
            low = top - (1 << bit)
            on = ((at >> bit) & 1) == 1
            part = jnp.zeros((HD, HD), F32)
            for i in range(size):
                take = jnp.logical_and(on, jnp.logical_and(i >= low, i < top))
                part = part + jnp.where(take, near[i], 0.0) * f[i]
            levels.append(part)
        if last:
            return levels
        whole = jnp.zeros((HD, HD), F32)
        for i in range(size):
            whole = whole + jnp.exp(total - ends[i]) * f[i]
        return levels, whole, start

    def keep(n, slot, value):
        h = 2 * c + n
        lower = fall[0, pl.ds(h, 1), :]
        rb[h, 1 + slot] = (value * jnp.where(c == 1, lower, 1.0)).astype(BF)
        rs[n, slot] = (value * jnp.where(c == 0, lower, 1.0)).astype(BF)

    offsets, y_copies = [], []
    for n in range(2):
        for cp, got in x_copies[n]:
            got.wait_recv()
        if n == 0:
            yd[y] = sum(xd[i] for i in range(X))
        levels, whole, start = weighted(xb, xd, n, x, X, 0.0, False)
        yb[y, n] = whole.astype(BF)
        y_copies.append(spread((yb, yd), y, Y, ys, yr, at_y, n))
        offsets.append(start)
        for bit in range(xbits):
            keep(n, bit, levels[bit])

    inside(2)
    inside(3)

    def w0_wait(n, carry):
        a, b = n // Z, lax.rem(n, Z)
        pltpu.make_async_copy(w_ref.at[0, 0], wb.at[y, x, c, a, b], w0r.at[a, b]).wait()
        return carry

    w1 = []

    def w1_pass():
        lax.fori_loop(0, 2 * Z, w0_wait, 0)
        for s in range(1, X):
            piece, dev = wb.at[y, x, c, 0], (at_x(s), z)
            cp = remote(piece, piece, w1s.at[0, s - 1], w1r.at[0, s - 1], dev)
            cp.start()
            there = wb.at[y, lax.rem(x + X - s, X), c, 0]
            w1.append((cp, remote(there, there, w1s.at[0, s - 1], w1r.at[0, s - 1], dev)))
        for s in range(1, Y):
            piece, dev = wb.at[y, x, c, 1], (at_y(s), z)
            cp = remote(piece, piece, w1s.at[1, s - 1], w1r.at[1, s - 1], dev)
            cp.start()
            there = wb.at[lax.rem(y + Y - s, Y), x, c, 1]
            w1.append((cp, remote(there, there, w1s.at[1, s - 1], w1r.at[1, s - 1], dev)))

    def travels(way, d, n):
        return d < H2 - 1 or (n < 2) == (way == 0)

    def ring(way, d, n):
        origin = lax.rem(z + (Z - d if way == 0 else d), Z)
        chunk = ab.at[origin, lax.rem(2 * c + n, HL)]
        dev = (me, right if way == 0 else left)
        return remote(chunk, chunk, rings.at[way, d, n], ringr.at[way, d, n], dev)

    def ring_got(way, d, n):
        origin = lax.rem(z + (Z - d - 1 if way == 0 else d + 1), Z)
        chunk = ab.at[origin, lax.rem(2 * c + n, HL)]
        dev = (me, right if way == 0 else left)
        return remote(chunk, chunk, rings.at[way, d, n], ringr.at[way, d, n], dev)

    def finish(h):
        for b in range(NB):
            rows = slice(b * BLOCK, (b + 1) * BLOCK)
            qf = qb[h, rows, :].astype(F32)
            lhs = jnp.concatenate(
                [(qf * col[h, :, b * 16 + 3 + n:b * 16 + 4 + n]).astype(BF) for n in range(NR)], axis=1
            )
            total = mix[h, rows, :] + jnp.dot(lhs, rb[h].reshape(NR * HD, HD), preferred_element_type=F32)
            mean = jnp.mean(total * total, axis=-1, keepdims=True)
            ab[z, h, rows, :] = (total * lax.rsqrt(mean + 1e-06)).astype(BF)

    def state_copy(n, h):
        return remote(rs.at[n], rb.at[h + n, pl.ds(1, NR - 1)], rss.at[n], rsr.at[n], mate)

    for n in range(HL):
        if n < 2:
            for cp, got in y_copies[n]:
                got.wait_recv()
            levels = weighted(yb, yd, n, y, Y, offsets[n], True)
            for bit in range(ybits):
                keep(n, xbits + bit, levels[bit])
            state_copy(n, 2 * c).start()
        else:
            state_copy(n - 2, 2 - 2 * c).wait_recv()
        finish(lax.rem(2 * c + n, HL))
        for way in range(2):
            if travels(way, 0, n):
                ring(way, 0, n).start()
    w1_pass()

    w2 = {}
    wc = []

    def block(axis, at, part, core):
        if axis == 0:
            return wb.at[at, :, core, 0] if part is None else wb.at[at, pl.ds(part * (X // 2), X // 2), core, 0]
        return wb.at[:, at, core, 1] if part is None else wb.at[pl.ds(part * (Y // 2), Y // 2), at, core, 1]

    def across(axis, at, part):
        n = len(wc)
        cp = remote(block(axis, at, part, c), block(axis, at, part, c), wcs.at[n], wcr.at[n], mate)
        cp.start()
        other = block(axis, at, part, 1 - c)
        wc.append((cp, remote(other, other, wcs.at[n], wcr.at[n], mate)))

    def near(axis, s):
        size, at = (Y, y) if axis == 0 else (X, x)
        return lax.rem(at + s + size, size)

    def w2_copy(axis, way, k):
        sign = 1 - 2 * way
        part = way if k != 1 else 1 - way
        dev = (at_y(sign % Y) if axis == 0 else at_x(sign % X), z)
        sems = (w2s.at[axis, way, k], w2r.at[axis, way, k])
        mine = block(axis, near(axis, 0 if k < 2 else -sign), part, c)
        at = near(axis, -sign if k < 2 else -2 * sign)
        theirs = block(axis, at, part, c)
        cp = remote(mine, mine, *sems, dev)
        cp.start()
        w2[axis, way, k] = (cp, remote(theirs, theirs, *sems, dev), at, part)

    def w2_pass():
        for cp, got in w1:
            got.wait_recv()
        for k in range(2):
            for axis in range(2):
                for way in range(2):
                    w2_copy(axis, way, k)
        across(0, y, None)
        across(1, x, None)

    def w3_pass(k):
        for axis in range(2):
            for way in range(2):
                _, got, at, part = w2[axis, way, k]
                got.wait_recv()
                if k == 0:
                    w2_copy(axis, way, 2)
                across(axis, at, part)

    def project(origins, first, last=False, heads=range(HL), shifted=False):
        for part in range(2):
            pick = [h if not shifted else lax.rem((y, x)[part] + h, HL) for h in heads]

            def tile(core, carry):
                u = 2 * part + core
                lhs = jnp.concatenate([ab[origin, h] for origin in origins for h in pick], axis=1)
                rhs = jnp.concatenate([
                    (wb[h, :, core, 0, origin] if part == 0 else wb[:, h, core, 1, origin]).reshape(HD, COLS)
                    for origin in origins for h in pick
                ], axis=0)
                total = jnp.dot(lhs, rhs, preferred_element_type=F32)
                if not first:
                    total = total + acc[u]
                if last:
                    ob[u] = total.astype(BF)
                    out_copy(u).start()
                else:
                    acc[u] = total
                return carry

            lax.fori_loop(0, 2, tile, 0)

    def out_copy(u):
        return pltpu.make_async_copy(ob.at[u], out_ref.at[:, pl.ds(pl.multiple_of(u * COLS, COLS), COLS)], out_sem.at[u])

    waiting = [[z]]
    behind = []
    begun = False
    for d in range(H2 - 1):
        for n in range(HL):
            for way in range(2):
                ring_got(way, d, n).wait_recv()
                if travels(way, d + 1, n):
                    ring(way, d + 1, n).start()
            slot = d * HL + n
            if slot == W2_SLOT:
                w2_pass()
            for k in range(3):
                if slot == W3_SLOTS[k]:
                    w3_pass(k)
            if slot == W3_SLOTS[1] + 1:
                for _, got in wc[:10]:
                    got.wait_recv()
            if W3_SLOTS[1] < slot <= W3_SLOTS[2] and waiting:
                project(waiting[0], not begun, False, (0, 1, 3), True)
                begun = True
                behind += waiting.pop(0)
            if slot == W3_SLOTS[2] + 1:
                for _, got in wc[10:]:
                    got.wait_recv()
                project(behind, False, False, (2,), True)
            elif slot > W3_SLOTS[2] and waiting:
                project(waiting.pop(0), False)
        waiting.append([lax.rem(z + Z - d - 1, Z), lax.rem(z + d + 1, Z)])
    while waiting:
        project(waiting.pop(0), False)
    for n in range(2):
        ring_got(0, H2 - 1, n).wait_recv()
        ring_got(1, H2 - 1, n + 2).wait_recv()
        project([lax.rem(z + H2, Z)], False, n == 1, (n, n + 2))

    def w0_sent(n, carry):
        @pl.when(jnp.logical_not(w0_place(n)[3]))
        def _():
            w0_copy(n).wait_send()

        return carry

    lax.fori_loop(0, R, w0_sent, 0)
    for cp in core_copies:
        cp.wait_send()
    for other in range(2):
        for step in range(Y):
            if other + step:
                wq_done(other, step).wait_send()
    for n in range(2):
        state_copy(n, 2 * c).wait_send()
    for cp, _ in x_copies[0] + x_copies[1] + y_copies[0] + y_copies[1] + w1 + wc + [(cp, 0) for cp, _, _, _ in w2.values()]:
        cp.wait_send()
    for way in range(2):
        for d in range(H2):
            for n in range(HL):
                if travels(way, d, n):
                    ring(way, d, n).wait_send()
    for u in range(4):
        out_copy(u).wait()


def local(X, Y, Z, queries, keys, values, log_decay, level_pick, level_table, out_weight):
    R = X * Y
    NR = 1 + (X.bit_length() - 1) + (Y.bit_length() - 1)
    H2 = Z // 2
    anyspace = pl.BlockSpec(memory_space=pl.ANY)
    dma = pltpu.SemaphoreType.DMA
    heads = (HL, TOK, HD)
    state = (HD, HD)
    scratch = [
        pltpu.VMEM((HL, TOK), F32), pltpu.VMEM((HL, TOK), jnp.int32), pltpu.VMEM(level_table.shape, F32),
        pltpu.VMEM(heads, BF), pltpu.VMEM(heads, BF), pltpu.VMEM(heads, BF),
        pltpu.VMEM((NB * HL, BLOCK), jnp.int32), pltpu.VMEM((NB * HL, BLOCK), F32), pltpu.VMEM((NB * HL, BLOCK), F32),
        pltpu.VMEM((HL, BLOCK, BLOCK), F32), pltpu.VMEM((BLOCK, BLOCK), F32),
        pltpu.VMEM(heads, F32),
        pltpu.VMEM((HL, 3) + state, BF),
        pltpu.VMEM((2, Y, 2, TOK // R, COLS), BF),
        pltpu.VMEM((HL,) + state, BF), pltpu.VMEM((HL,) + state, BF),
        pltpu.VMEM((8, BLOCK), F32), pltpu.VMEM((8, BLOCK), F32), pltpu.VMEM((2, 8, BLOCK), F32),
        pltpu.VMEM((X, 2) + state, BF), pltpu.VMEM((X, 8, BLOCK), F32),
        pltpu.VMEM((Y, 2) + state, BF), pltpu.VMEM((Y, 8, BLOCK), F32),
        pltpu.VMEM((2, NR - 1) + state, BF), pltpu.VMEM((HL, NR) + state, BF),
        pltpu.VMEM((Z,) + heads, BF),
        pltpu.VMEM((Y, X, 2, 2, Z, TOK // R, COLS), BF),
        pltpu.VMEM((4, TOK, COLS), F32), pltpu.VMEM((4, TOK, COLS), BF),
        dma((4, HL)), dma((4,)),
        dma((2, Y)), dma((2, Y)),
        dma((R,)), dma((2, Z)),
        dma((2, max(X, Y))), dma((2, max(X, Y))),
        dma((2, 2, 3)), dma((2, 2, 3)),
        dma((14,)), dma((14,)),
        dma((2,)), dma((2,)),
        dma((X, 3)), dma((X, 3)),
        dma((Y, 3)), dma((Y, 3)),
        dma((2,)), dma((2,)),
        dma((2, H2, HL)), dma((2, H2, HL)),
        pltpu.SemaphoreType.REGULAR((2,)),
    ]
    return pl.pallas_call(
        functools.partial(kernel, X, Y, Z),
        out_shape=jax.ShapeDtypeStruct((TOK, 4 * COLS), BF),
        in_specs=[anyspace] * 7,
        out_specs=anyspace,
        scratch_shapes=scratch,
        cost_estimate=pl.CostEstimate(flops=5_000_000_000, bytes_accessed=4_000_000, transcendentals=1_000_000),
        compiler_params=pltpu.CompilerParams(
            collective_id=0, has_side_effects=True, vmem_limit_bytes=61 * 1024 * 1024
        ),
    )(queries, keys, values, log_decay, level_pick, level_table, out_weight.reshape(Y, X, TOK // R, COLS))


def solution(mesh):
    nctx, Z = mesh.shape["ctx"], mesh.shape["head"]
    chips = nctx // 2
    X = 1 << int(math.log2(chips)) // 2
    Y = chips // X
    in_specs = (
        P("ctx", "head"),
        P("ctx", "head"),
        P("ctx", "head"),
        P("head", "ctx"),
        P("head", "ctx"),
        P("head", None, None),
        P("head", "ctx"),
    )
    return jax.shard_map(
        functools.partial(local, X, Y, Z), mesh=mesh, in_specs=in_specs, out_specs=P("ctx", "head"), check_vma=False
    )
```

```python
import functools
import math

import jax
import jax.numpy as jnp
from jax import lax
from jax.experimental import pallas as pl
from jax.experimental.pallas import tpu as pltpu
from jax.sharding import PartitionSpec as P

HD = 128
BLOCK = 128
HL = 4
TOK = 512
NB = TOK // BLOCK
COLS = 256
W2_SLOT, W3_SLOTS = 1, (4, 6, 9)
MESH = pl.DeviceIdType.MESH
BF = jnp.bfloat16
F32 = jnp.float32


def kernel(
    X, Y, Z,
    q_ref, k_ref, v_ref, ld_hbm, pick_hbm, table_hbm, w_ref, out_ref,
    ld_ref, pick_ref, table_ref,
    qb, kb, vb, picks, wrows, bdrows, col, kcol, mix, lst, stage, t0, t0p, d0, d0p, fall, xb, xd, yb, yd, rs, rb, ab, wb, acc,
    in_sem, wqs, wqr, w0s, w0r, w1s, w1r, w2s, w2r, wcs, wcr, cs, cr, xs, xr, ys, yr, rss, rsr, rings, ringr, relay_sem,
):
    R = X * Y
    RP = TOK // R
    xbits = X.bit_length() - 1
    ybits = Y.bit_length() - 1
    NR = 1 + xbits + ybits
    H2 = Z // 2
    me = lax.axis_index("ctx")
    z = lax.axis_index("head")
    c = lax.rem(me, 2)
    chip = me // 2
    x = lax.rem(chip, X)
    y = chip // X
    half = lax.rem(x, 2)
    mate = (me + 1 - 2 * c, z)
    right = lax.rem(z + 1, Z)
    left = lax.rem(z + Z - 1, Z)

    def at_x(step):
        return (y * X + lax.rem(x + step, X)) * 2 + c

    def at_y(step):
        return (lax.rem(y + step, Y) * X + x) * 2 + c

    def remote(src, dst, ssem, rsem, dev):
        return pltpu.make_async_remote_copy(
            src_ref=src, dst_ref=dst, send_sem=ssem, recv_sem=rsem, device_id=dev, device_id_type=MESH
        )

    barrier = pltpu.get_barrier_semaphore()

    def greet(ctx, head):
        pl.semaphore_signal(barrier, inc=1, device_id=(ctx, head), device_id_type=MESH)

    greet(mate[0], z)
    for s in range(1, X):
        greet(at_x(s), z)
    for s in range(1, Y):
        greet(at_y(s), z)
    for s in range(1, Y):
        greet((lax.rem(y + s, Y) * X + lax.rem(x + 2, X)) * 2 + c, z)
    for s in (1, 2, Z - 2, Z - 1):
        greet(me, lax.rem(z + s, Z))


    small = [
        pltpu.make_async_copy(src, dst, in_sem.at[3, n])
        for n, (src, dst) in enumerate(((ld_hbm, ld_ref), (pick_hbm, pick_ref), (table_hbm, table_ref)))
    ]
    for cp in small:
        cp.start()
    loads = []
    for n, (src, dst) in enumerate(((k_ref, kb), (v_ref, vb), (q_ref, qb))):
        for h in range(HL):
            cp = pltpu.make_async_copy(src.at[:, h * HD:(h + 1) * HD], dst.at[h], in_sem.at[n, h])
            cp.start()
            loads.append(cp)

    for cp in small:
        cp.wait()

    for b in range(NB):
        wrows[b * HL:(b + 1) * HL, :] = ld_ref[:, b * BLOCK:(b + 1) * BLOCK]
        picks[b * HL:(b + 1) * HL, :] = pick_ref[:, b * BLOCK:(b + 1) * BLOCK]
    run = wrows[...]
    lane = lax.broadcasted_iota(jnp.int32, run.shape, 1)
    step = 1
    while step < BLOCK:
        run = run + jnp.where(lane >= step, pltpu.roll(run, step, 1), 0.0)
        step *= 2
    wrows[...] = run
    bdrows[...] = jnp.broadcast_to(run[:, BLOCK - 1:BLOCK], run.shape)
    scale = jnp.exp(bdrows[...] - run)
    kcol[...] = jnp.concatenate([scale, jnp.zeros((BLOCK - NB * HL, BLOCK), F32)], axis=0).T
    d0[...] = jnp.zeros_like(d0)
    d0[0:HL, :] = sum(bdrows[b * HL:(b + 1) * HL, :] for b in range(NB))

    for cp in loads[:2 * HL]:
        cp.wait()

    for h in range(HL):
        s = []
        for b in range(NB):
            kk = kb[h, b * BLOCK:(b + 1) * BLOCK, :].astype(F32)
            kk = (kk * kcol[:, b * HL + h:b * HL + h + 1]).astype(BF)
            s.append(lax.dot_general(
                kk, vb[h, b * BLOCK:(b + 1) * BLOCK, :], (((0,), (0,)), ((), ())), preferred_element_type=F32
            ))
        e = [jnp.exp(bdrows[b * HL + h:b * HL + h + 1, :]) for b in range(NB)]
        pair = e[1] * s[0] + s[1]
        lst[h, 0] = s[0].astype(BF)
        lst[h, 1] = pair.astype(BF)
        lst[h, 2] = s[2].astype(BF)
        t0[h] = (e[3] * (e[2] * pair + s[2]) + s[3]).astype(BF)

    pl.semaphore_wait(barrier, 1 + (X - 1) + 2 * (Y - 1) + 4)

    core_copies = [
        remote(t0, t0p, cs.at[0], cr.at[0], mate),
        remote(d0, d0p, cs.at[1], cr.at[1], mate),
    ]
    for cp in core_copies:
        cp.start()

    beside = x + 1 - 2 * lax.rem(x, 2)

    def relay(turn):
        if turn > 0:
            pl.semaphore_wait(relay_sem.at[turn - 1], 4 if turn == 1 else 1)
        if turn == 0:
            for s in (1, 2, Z - 2, Z - 1):
                pl.semaphore_signal(
                    relay_sem.at[0], inc=1, device_id=(me, lax.rem(z + s, Z)), device_id_type=MESH
                )
        elif turn == 1:
            pl.semaphore_signal(
                relay_sem.at[1], inc=1, device_id=((y * X + beside) * 2 + c, z), device_id_type=MESH
            )

    relay(0)

    far = lax.rem(x + 2, X)

    def spread_to(other, step):
        return ((lax.rem(y + step, Y) * X + (far if other else x)) * 2 + c, z)

    def wq_move(other, step):
        group = 1 - x // 2 if other else x // 2
        pair, row = pl.ds(2 * group, 2), lax.rem(y + step, Y)
        for way in range(2):
            @pl.when(half == way)
            def _():
                src = w_ref.at[row, pair] if way == 0 else w_ref.at[pair, row]
                dst = stage.at[x // 2, y]
                if not other and step == 0:
                    pltpu.make_async_copy(src, dst, wqr.at[0, 0]).start()
                else:
                    remote(src, dst, wqs.at[other, step], wqr.at[other, step], spread_to(other, step)).start()

    def wq_done(other, step):
        src, dst = w_ref.at[0, pl.ds(0, 2)], stage.at[1 - x // 2 if other else x // 2, lax.rem(y + Y - step, Y)]
        if not other and step == 0:
            return pltpu.make_async_copy(src, dst, wqr.at[0, 0])
        return remote(src, dst, wqs.at[other, step], wqr.at[other, step], spread_to(other, step))

    def w0_place(n):
        plane, low = lax.rem(n // 2 + z, Z), lax.rem(n + x, 2)
        col_at = x // 2 * 2 + low
        return plane, low, col_at, jnp.logical_and(plane == z, col_at == x)

    def w0_copy(n):
        plane, low, col_at, _ = w0_place(n)
        return remote(
            stage.at[lax.rem(plane, 2), plane // 2, low],
            wb.at[y, col_at, c, half, z],
            w0s.at[n], w0r.at[half, z], ((y * X + col_at) * 2 + c, plane),
        )

    def w0_send(n, carry):
        plane, low, col_at, own = w0_place(n)

        @pl.when(own)
        def _():
            pltpu.make_async_copy(
                stage.at[lax.rem(plane, 2), plane // 2, low],
                wb.at[y, col_at, c, half, z], w0r.at[half, z],
            ).start()

        @pl.when(jnp.logical_not(own))
        def _():
            w0_copy(n).start()

        return carry

    def w0_pass():
        for other in range(2):
            for step in range(Y):
                if other + step == 0:
                    wq_done(0, 0).wait()
                else:
                    wq_done(other, step).wait_recv()
        lax.fori_loop(0, R, w0_send, 0)

    for step in range(Y):
        wq_move(0, step)
        wq_move(1, step)

    for cp in loads[2 * HL:]:
        cp.wait()
    causal = (
        lax.broadcasted_iota(jnp.int32, (BLOCK, BLOCK), 0) >= lax.broadcasted_iota(jnp.int32, (BLOCK, BLOCK), 1)
    )

    def inside(h):
        for b in range(NB):
            rows = slice(b * BLOCK, (b + 1) * BLOCK)
            qq = qb[h, rows, :]
            score = lax.dot_general(
                qq, kb[h, rows, :], (((1,), (1,)), ((), ())), preferred_element_type=F32
            )
            gap = col[h, :, b * 16 + 8:b * 16 + 9] - wrows[pl.ds(b * HL + h, 1), :]
            decay = jnp.where(causal, jnp.exp(jnp.where(causal, gap, 0.0)), 0.0)
            lhs = [(col[h, :, b * 16:b * 16 + 1] * decay * score).astype(BF)]
            rhs = [vb[h, rows, :]]
            qf = qq.astype(F32)
            if b & 1:
                lhs.append((qf * col[h, :, b * 16 + 1:b * 16 + 2]).astype(BF))
                rhs.append(lst[h, b - 1])
            if b & 2:
                lhs.append((qf * col[h, :, b * 16 + 2:b * 16 + 3]).astype(BF))
                rhs.append(lst[h, 1])
            mix[h, rows, :] = jnp.dot(
                jnp.concatenate(lhs, axis=1), jnp.concatenate(rhs, axis=0), preferred_element_type=F32
            )

    for cp in core_copies:
        cp.wait_recv()
    fall[0] = jnp.exp(jnp.where(c == 0, d0[...], d0p[...]))
    fall[1] = jnp.exp(jnp.where(c == 0, d0p[...], d0[...]))
    xd[x] = d0[...] + d0p[...]

    def spread(bufs, at, size, ssem, rsem, dev_of, n):
        copies = []
        state, decays = bufs
        for s in range(1, size):
            src = lax.rem(at + size - s, size)
            pieces = [(state.at[at, n], state.at[src, n], n)]
            if n == 0:
                pieces.append((decays.at[at], decays.at[src], 2))
            for mine, theirs, i in pieces:
                cp = remote(mine, mine, ssem.at[s - 1, i], rsem.at[s - 1, i], (dev_of(s), z))
                cp.start()
                copies.append((cp, remote(theirs, theirs, ssem.at[s - 1, i], rsem.at[s - 1, i], (dev_of(s), z))))
        return copies

    x_copies = []
    for n in range(2):
        h = 2 * c + n
        sec = fall[1, pl.ds(h, 1), :]
        mine = t0[h].astype(F32) * jnp.where(c == 0, sec, 1.0)
        other = t0p[h].astype(F32) * jnp.where(c == 0, 1.0, sec)
        xb[x, n] = (mine + other).astype(BF)
        x_copies.append(spread((xb, xd), x, X, xs, xr, at_x, n))
    relay(1)
    sub = lax.broadcasted_iota(jnp.int32, (8, BLOCK), 0)

    def prepare(h, carry):
        tab = table_ref[h]
        bd = [bdrows[pl.ds(b * HL + h, 1), :] for b in range(NB)]
        start = jnp.zeros_like(bd[0])
        rows = []
        for b in range(NB):
            pk = jnp.broadcast_to(picks[pl.ds(b * HL + h, 1), :], (8, BLOCK))
            lw = jnp.zeros((8, BLOCK), F32)
            for n in range(16):
                lw = jnp.where(pk == n, tab[:, n:n + 1], lw)
            wr = wrows[pl.ds(b * HL + h, 1), :]
            upper = jnp.where(sub >= 3, start, 0.0)
            if b == 3:
                upper = jnp.where(sub == 2, bd[2], upper)
            rows.append(lw * jnp.where(sub == 0, 1.0, jnp.exp(wr + upper)))
            rows.append(jnp.where(sub == 0, wr, 0.0))
            start = start + bd[b]
        rows.append(jnp.zeros((BLOCK - 16 * NB, BLOCK), F32))
        col[h] = jnp.concatenate(rows, axis=0).T
        return carry

    lax.fori_loop(0, HL, prepare, 0)

    for h in range(HL):
        rb[h, 0] = jnp.where(c == 1, t0p[h].astype(F32), 0.0).astype(BF)

    inside(0)
    relay(2)
    w0_pass()
    inside(1)

    def weighted(buf, dec, n, at, size, before, last):
        h = 2 * c + n
        d = [dec[i, pl.ds(h, 1), :] for i in range(size)]
        ends, total = [], jnp.zeros_like(d[0])
        start = jnp.zeros_like(d[0])
        for i in range(size):
            start = start + jnp.where(i < at, d[i], 0.0)
            total = total + d[i]
            ends.append(total)
        f = [buf[i, n].astype(F32) for i in range(size)]
        near = [jnp.exp(jnp.minimum(start - ends[i], 0.0) + before) for i in range(size)]
        levels = []
        for bit in range(size.bit_length() - 1):
            top = (at >> bit) << bit
            low = top - (1 << bit)
            on = ((at >> bit) & 1) == 1
            part = jnp.zeros((HD, HD), F32)
            for i in range(size):
                take = jnp.logical_and(on, jnp.logical_and(i >= low, i < top))
                part = part + jnp.where(take, near[i], 0.0) * f[i]
            levels.append(part)
        if last:
            return levels
        whole = jnp.zeros((HD, HD), F32)
        for i in range(size):
            whole = whole + jnp.exp(total - ends[i]) * f[i]
        return levels, whole, start

    def keep(n, slot, value):
        h = 2 * c + n
        lower = fall[0, pl.ds(h, 1), :]
        rb[h, 1 + slot] = (value * jnp.where(c == 1, lower, 1.0)).astype(BF)
        rs[n, slot] = (value * jnp.where(c == 0, lower, 1.0)).astype(BF)

    offsets, y_copies = [], []
    for n in range(2):
        for cp, got in x_copies[n]:
            got.wait_recv()
        if n == 0:
            yd[y] = sum(xd[i] for i in range(X))
        levels, whole, start = weighted(xb, xd, n, x, X, 0.0, False)
        yb[y, n] = whole.astype(BF)
        y_copies.append(spread((yb, yd), y, Y, ys, yr, at_y, n))
        offsets.append(start)
        for bit in range(xbits):
            keep(n, bit, levels[bit])

    inside(2)
    inside(3)

    def w0_wait(n, carry):
        a, b = n // Z, lax.rem(n, Z)
        pltpu.make_async_copy(w_ref.at[0, 0], wb.at[y, x, c, a, b], w0r.at[a, b]).wait()
        return carry

    w1 = []

    def w1_pass():
        lax.fori_loop(0, 2 * Z, w0_wait, 0)
        for s in range(1, X):
            piece, dev = wb.at[y, x, c, 0], (at_x(s), z)
            cp = remote(piece, piece, w1s.at[0, s - 1], w1r.at[0, s - 1], dev)
            cp.start()
            there = wb.at[y, lax.rem(x + X - s, X), c, 0]
            w1.append((cp, remote(there, there, w1s.at[0, s - 1], w1r.at[0, s - 1], dev)))
        for s in range(1, Y):
            piece, dev = wb.at[y, x, c, 1], (at_y(s), z)
            cp = remote(piece, piece, w1s.at[1, s - 1], w1r.at[1, s - 1], dev)
            cp.start()
            there = wb.at[lax.rem(y + Y - s, Y), x, c, 1]
            w1.append((cp, remote(there, there, w1s.at[1, s - 1], w1r.at[1, s - 1], dev)))

    def travels(way, d, n):
        return d < H2 - 1 or (n < 2) == (way == 0)

    def ring(way, d, n):
        origin = lax.rem(z + (Z - d if way == 0 else d), Z)
        chunk = ab.at[origin, lax.rem(2 * c + n, HL)]
        dev = (me, right if way == 0 else left)
        return remote(chunk, chunk, rings.at[way, d, n], ringr.at[way, d, n], dev)

    def ring_got(way, d, n):
        origin = lax.rem(z + (Z - d - 1 if way == 0 else d + 1), Z)
        chunk = ab.at[origin, lax.rem(2 * c + n, HL)]
        dev = (me, right if way == 0 else left)
        return remote(chunk, chunk, rings.at[way, d, n], ringr.at[way, d, n], dev)

    def finish(h):
        for b in range(NB):
            rows = slice(b * BLOCK, (b + 1) * BLOCK)
            qf = qb[h, rows, :].astype(F32)
            lhs = jnp.concatenate(
                [(qf * col[h, :, b * 16 + 3 + n:b * 16 + 4 + n]).astype(BF) for n in range(NR)], axis=1
            )
            total = mix[h, rows, :] + jnp.dot(lhs, rb[h].reshape(NR * HD, HD), preferred_element_type=F32)
            mean = jnp.mean(total * total, axis=-1, keepdims=True)
            ab[z, h, rows, :] = (total * lax.rsqrt(mean + 1e-06)).astype(BF)

    def state_copy(n, h):
        return remote(rs.at[n], rb.at[h + n, pl.ds(1, NR - 1)], rss.at[n], rsr.at[n], mate)

    for n in range(HL):
        if n < 2:
            for cp, got in y_copies[n]:
                got.wait_recv()
            levels = weighted(yb, yd, n, y, Y, offsets[n], True)
            for bit in range(ybits):
                keep(n, xbits + bit, levels[bit])
            state_copy(n, 2 * c).start()
        else:
            state_copy(n - 2, 2 - 2 * c).wait_recv()
        finish(lax.rem(2 * c + n, HL))
        for way in range(2):
            if travels(way, 0, n):
                ring(way, 0, n).start()
    w1_pass()

    w2 = {}
    wc = []

    def block(axis, at, part, core):
        if axis == 0:
            return wb.at[at, :, core, 0] if part is None else wb.at[at, pl.ds(part * (X // 2), X // 2), core, 0]
        return wb.at[:, at, core, 1] if part is None else wb.at[pl.ds(part * (Y // 2), Y // 2), at, core, 1]

    def across(axis, at, part):
        n = len(wc)
        cp = remote(block(axis, at, part, c), block(axis, at, part, c), wcs.at[n], wcr.at[n], mate)
        cp.start()
        other = block(axis, at, part, 1 - c)
        wc.append((cp, remote(other, other, wcs.at[n], wcr.at[n], mate)))

    def near(axis, s):
        size, at = (Y, y) if axis == 0 else (X, x)
        return lax.rem(at + s + size, size)

    def w2_copy(axis, way, k):
        sign = 1 - 2 * way
        part = way if k != 1 else 1 - way
        dev = (at_y(sign % Y) if axis == 0 else at_x(sign % X), z)
        sems = (w2s.at[axis, way, k], w2r.at[axis, way, k])
        mine = block(axis, near(axis, 0 if k < 2 else -sign), part, c)
        at = near(axis, -sign if k < 2 else -2 * sign)
        theirs = block(axis, at, part, c)
        cp = remote(mine, mine, *sems, dev)
        cp.start()
        w2[axis, way, k] = (cp, remote(theirs, theirs, *sems, dev), at, part)

    def w2_pass():
        for cp, got in w1:
            got.wait_recv()
        for k in range(2):
            for axis in range(2):
                for way in range(2):
                    w2_copy(axis, way, k)
        across(0, y, None)
        across(1, x, None)

    def w3_pass(k):
        for axis in range(2):
            for way in range(2):
                _, got, at, part = w2[axis, way, k]
                got.wait_recv()
                if k == 0:
                    w2_copy(axis, way, 2)
                across(axis, at, part)

    def project(origins, first, last=False, heads=range(HL), shifted=False):
        for part in range(2):
            pick = [h if not shifted else lax.rem((y, x)[part] + h, HL) for h in heads]

            def tile(core, carry):
                u = 2 * part + core
                lhs = jnp.concatenate([ab[origin, h] for origin in origins for h in pick], axis=1)
                rhs = jnp.concatenate([
                    (wb[h, :, core, 0, origin] if part == 0 else wb[:, h, core, 1, origin]).reshape(HD, COLS)
                    for origin in origins for h in pick
                ], axis=0)
                total = jnp.dot(lhs, rhs, preferred_element_type=F32)
                if not first:
                    total = total + acc[u]
                if last:
                    out_ref[:, pl.ds(pl.multiple_of(u * COLS, COLS), COLS)] = total.astype(BF)
                else:
                    acc[u] = total
                return carry

            lax.fori_loop(0, 2, tile, 0)

    waiting = [[z]]
    behind = []
    begun = False
    for d in range(H2 - 1):
        for n in range(HL):
            for way in range(2):
                ring_got(way, d, n).wait_recv()
                if travels(way, d + 1, n):
                    ring(way, d + 1, n).start()
            slot = d * HL + n
            if slot == W2_SLOT:
                w2_pass()
            for k in range(3):
                if slot == W3_SLOTS[k]:
                    w3_pass(k)
            if slot == W3_SLOTS[1] + 1:
                for _, got in wc[:10]:
                    got.wait_recv()
            if W3_SLOTS[1] < slot <= W3_SLOTS[2] and waiting:
                project(waiting[0], not begun, False, (0, 1, 3), True)
                begun = True
                behind += waiting.pop(0)
            if slot == W3_SLOTS[2] + 1:
                for _, got in wc[10:]:
                    got.wait_recv()
                project(behind, False, False, (2,), True)
            elif slot > W3_SLOTS[2] and waiting:
                project(waiting.pop(0), False)
        waiting.append([lax.rem(z + Z - d - 1, Z), lax.rem(z + d + 1, Z)])
    while waiting:
        project(waiting.pop(0), False)
    for n in range(2):
        ring_got(0, H2 - 1, n).wait_recv()
        ring_got(1, H2 - 1, n + 2).wait_recv()
        project([lax.rem(z + H2, Z)], False, n == 1, (n, n + 2))

    def w0_sent(n, carry):
        @pl.when(jnp.logical_not(w0_place(n)[3]))
        def _():
            w0_copy(n).wait_send()

        return carry

    lax.fori_loop(0, R, w0_sent, 0)
    for cp in core_copies:
        cp.wait_send()
    for other in range(2):
        for step in range(Y):
            if other + step:
                wq_done(other, step).wait_send()
    for n in range(2):
        state_copy(n, 2 * c).wait_send()
    for cp, _ in x_copies[0] + x_copies[1] + y_copies[0] + y_copies[1] + w1 + wc + [(cp, 0) for cp, _, _, _ in w2.values()]:
        cp.wait_send()
    for way in range(2):
        for d in range(H2):
            for n in range(HL):
                if travels(way, d, n):
                    ring(way, d, n).wait_send()


def local(X, Y, Z, queries, keys, values, log_decay, level_pick, level_table, out_weight):
    R = X * Y
    NR = 1 + (X.bit_length() - 1) + (Y.bit_length() - 1)
    H2 = Z // 2
    anyspace = pl.BlockSpec(memory_space=pl.ANY)
    dma = pltpu.SemaphoreType.DMA
    heads = (HL, TOK, HD)
    state = (HD, HD)
    scratch = [
        pltpu.VMEM((HL, TOK), F32), pltpu.VMEM((HL, TOK), jnp.int32), pltpu.VMEM(level_table.shape, F32),
        pltpu.VMEM(heads, BF), pltpu.VMEM(heads, BF), pltpu.VMEM(heads, BF),
        pltpu.VMEM((NB * HL, BLOCK), jnp.int32), pltpu.VMEM((NB * HL, BLOCK), F32), pltpu.VMEM((NB * HL, BLOCK), F32),
        pltpu.VMEM((HL, BLOCK, BLOCK), F32), pltpu.VMEM((BLOCK, BLOCK), F32),
        pltpu.VMEM(heads, F32),
        pltpu.VMEM((HL, 3) + state, BF),
        pltpu.VMEM((2, Y, 2, TOK // R, COLS), BF),
        pltpu.VMEM((HL,) + state, BF), pltpu.VMEM((HL,) + state, BF),
        pltpu.VMEM((8, BLOCK), F32), pltpu.VMEM((8, BLOCK), F32), pltpu.VMEM((2, 8, BLOCK), F32),
        pltpu.VMEM((X, 2) + state, BF), pltpu.VMEM((X, 8, BLOCK), F32),
        pltpu.VMEM((Y, 2) + state, BF), pltpu.VMEM((Y, 8, BLOCK), F32),
        pltpu.VMEM((2, NR - 1) + state, BF), pltpu.VMEM((HL, NR) + state, BF),
        pltpu.VMEM((Z,) + heads, BF),
        pltpu.VMEM((Y, X, 2, 2, Z, TOK // R, COLS), BF),
        pltpu.VMEM((4, TOK, COLS), F32),
        dma((4, HL)),
        dma((2, Y)), dma((2, Y)),
        dma((R,)), dma((2, Z)),
        dma((2, max(X, Y))), dma((2, max(X, Y))),
        dma((2, 2, 3)), dma((2, 2, 3)),
        dma((14,)), dma((14,)),
        dma((2,)), dma((2,)),
        dma((X, 3)), dma((X, 3)),
        dma((Y, 3)), dma((Y, 3)),
        dma((2,)), dma((2,)),
        dma((2, H2, HL)), dma((2, H2, HL)),
        pltpu.SemaphoreType.REGULAR((2,)),
    ]
    operands = (
        queries, keys, values, log_decay, level_pick, level_table, out_weight.reshape(Y, X, TOK // R, COLS)
    )
    return pl.pallas_call(
        functools.partial(kernel, X, Y, Z),
        out_shape=jax.ShapeDtypeStruct((TOK, 4 * COLS), BF),
        in_specs=[anyspace] * 7,
        out_specs=pl.BlockSpec(memory_space=pltpu.VMEM),
        scratch_shapes=scratch,
        cost_estimate=pl.CostEstimate(flops=5_000_000_000, bytes_accessed=4_000_000, transcendentals=1_000_000),
        compiler_params=pltpu.CompilerParams(
            collective_id=0, has_side_effects=True, vmem_limit_bytes=48 * 1024 * 1024
        ),
    )(*[pltpu.with_memory_space_constraint(a, pltpu.HBM) for a in operands])


def solution(mesh):
    nctx, Z = mesh.shape["ctx"], mesh.shape["head"]
    chips = nctx // 2
    X = 1 << int(math.log2(chips)) // 2
    Y = chips // X
    in_specs = (
        P("ctx", "head"),
        P("ctx", "head"),
        P("ctx", "head"),
        P("head", "ctx"),
        P("head", "ctx"),
        P("head", None, None),
        P("head", "ctx"),
    )
    return jax.shard_map(
        functools.partial(local, X, Y, Z), mesh=mesh, in_specs=in_specs, out_specs=P("ctx", "head"), check_vma=False
    )
```
